256 devices in a mesh: row: 16 (over y, x), col: 16 (over z, core).
Axes of the slice: x: 4, y: 4, z: 8, core: 2. Of those that a mesh axis runs over, the one named last changes fastest.
Arguments:
- queries: bfloat16 [256, 256, 768], P('row', 'col'), may hold values from -15 to 15
- keys: bfloat16 [256, 256, 768], P('row', 'col'), may hold values from -15 to 15
- values: bfloat16 [256, 256, 768], P('row', 'col'), may hold values from -6 to 6
- list_one: int32 [256, 27], replicated, may hold values from -1 to 255, as said below
- list_two: int32 [64, 27], replicated, may hold values from -1 to 63, as said below
Outputs:
- attended: bfloat16 [256, 256, 768], P('row', 'col')
The draws below stay inside these ranges and needn't reach their ends.
Inputs may be any that keep to these rules, and one draw needn't show every extreme that they name: `list_one`: row b names level-1 blocks (16 x 16 tokens, numbered row-major) that block b interacts with; each entry is -1 or a child of one of the 3 x 3 neighbours of b's parent block that is not among b's own 3 x 3 neighbours, so its block row and column lie within 3 of b's; no block appears twice in a row. `list_two`: row b names level-2 blocks (32 x 32 tokens, numbered row-major) that block b interacts with; each entry is -1 or a block other than b whose block row and column lie within 3 of b's; no block appears twice in a row.
All inputs are finite; a program needn't handle non-finite values.
Results may differ from the reference program's by a relative error of at most 0.0054.
Values may be sent and summed in bfloat16 or wider, within the bound.
No kernel may reach another device: no remote copies, remote signals or barrier semaphores. Data moves between devices by JAX's collectives and lax.ppermute only.
A program may use at most 128 MiB of HBM per device.

```python
import math
import jax
import jax.numpy as jnp
from jax import lax

D = 768
HEADS = 12
TILE = 16
IMG_R = 256
IMG_C = 256


def draw_queries(key, part):
    key = jax.random.fold_in(key, 1)
    drawn = jnp.clip(jax.random.normal(key, (IMG_R, IMG_C, D), jnp.float32), -4.0, 4.0)
    return drawn.astype(jnp.bfloat16)


def draw_keys(key, part):
    key = jax.random.fold_in(key, 2)
    drawn = jnp.clip(jax.random.normal(key, (IMG_R, IMG_C, D), jnp.float32), -4.0, 4.0)
    return drawn.astype(jnp.bfloat16)


def interaction_list(key, block_rows, block_cols):
    count = block_rows * block_cols
    block_index = jnp.arange(count, dtype=jnp.int32)
    own_row = (block_index // block_cols)[:, None]
    own_col = (block_index % block_cols)[:, None]
    offsets = jnp.arange(36, dtype=jnp.int32)[None, :]
    cand_rows = 2 * (own_row // 2) - 2 + offsets // 6
    cand_cols = 2 * (own_col // 2) - 2 + offsets % 6
    adjacent = (jnp.abs(cand_rows - own_row) <= 1) & (jnp.abs(cand_cols - own_col) <= 1)
    order = jnp.argsort(adjacent.astype(jnp.int32), axis=1, stable=True)[:, :27]
    sel_rows = jnp.take_along_axis(cand_rows, order, axis=1)
    sel_cols = jnp.take_along_axis(cand_cols, order, axis=1)
    within = (sel_rows >= 0) & (sel_rows < block_rows) & (sel_cols >= 0) & (sel_cols < block_cols)
    keep = jax.random.randint(jax.random.fold_in(key, 7), (count, 27), 0, 8) > 0
    entries = jnp.where(within & keep, sel_rows * block_cols + sel_cols, -1).astype(jnp.int32)
    shuffle = jax.random.randint(jax.random.fold_in(key, 9), (count, 27), 0, 1 << 20) * 32 + jnp.arange(27, dtype=jnp.int32)[None, :]
    return jnp.take_along_axis(entries, jnp.argsort(shuffle, axis=1, stable=True), axis=1)


def top_list(key, block_rows, block_cols):
    count = block_rows * block_cols
    block_index = jnp.arange(count, dtype=jnp.int32)
    own_row = (block_index // block_cols)[:, None]
    own_col = (block_index % block_cols)[:, None]
    offsets = jnp.arange(48, dtype=jnp.int32)[None, :]
    spots = offsets + (offsets >= 24).astype(jnp.int32)
    cand_rows = own_row + spots // 7 - 3
    cand_cols = own_col + spots % 7 - 3
    within = (cand_rows >= 0) & (cand_rows < block_rows) & (cand_cols >= 0) & (cand_cols < block_cols)
    ranking = (1 - within.astype(jnp.int32)) * (1 << 27) + jax.random.randint(jax.random.fold_in(key, 5), (count, 48), 0, 1 << 20) * 64 + offsets
    order = jnp.argsort(ranking, axis=1, stable=True)[:, :27]
    sel_rows = jnp.take_along_axis(cand_rows, order, axis=1)
    sel_cols = jnp.take_along_axis(cand_cols, order, axis=1)
    sel_ok = (sel_rows >= 0) & (sel_rows < block_rows) & (sel_cols >= 0) & (sel_cols < block_cols)
    keep = jax.random.randint(jax.random.fold_in(key, 7), (count, 27), 0, 8) > 0
    entries = jnp.where(sel_ok & keep, sel_rows * block_cols + sel_cols, -1).astype(jnp.int32)
    shuffle = jax.random.randint(jax.random.fold_in(key, 9), (count, 27), 0, 1 << 20) * 32 + jnp.arange(27, dtype=jnp.int32)[None, :]
    return jnp.take_along_axis(entries, jnp.argsort(shuffle, axis=1, stable=True), axis=1)


def draw_list_one(key, part):
    key = jax.random.fold_in(key, 11)
    return interaction_list(key, IMG_R // 16, IMG_C // 16)


def draw_list_two(key, part):
    key = jax.random.fold_in(key, 12)
    return top_list(key, IMG_R // 32, IMG_C // 32)


def block_levels(rng, extent, pieces, low, largest):
    gain, own = 1.0, jax.random.fold_in(rng, 6)
    for position, parts in pieces:
        steps = jnp.exp(jax.random.uniform(jax.random.fold_in(own, position), (parts,), jnp.float32, low / len(pieces), largest / len(pieces)))
        gain = gain * jnp.repeat(steps, extent[position] // parts).reshape([-1 if axis == position else 1 for axis in range(len(extent))])
    return gain


def noise(rng, dims, spread, most, split=(), kind=jnp.bfloat16):
    factor_of = block_levels(rng, dims, split, -0.22, 0.18) if split else 1.0
    array = jax.random.normal(rng, dims, jnp.float32) * spread * factor_of
    return jnp.minimum(jnp.maximum(array, -most), most).astype(kind)


def setup_inputs(seed: int = 0) -> dict:
    seeds = jax.random.split(jax.random.key(seed), 6)
    return {
        "queries": draw_queries(jax.random.fold_in(seeds[5], 71), 0),
        "keys": draw_keys(jax.random.fold_in(seeds[5], 71), 0),
        "values": noise(seeds[2], (IMG_R, IMG_C, D), 1.0, 6.0, ((0, 16), (1, 16))),
        "list_one": draw_list_one(jax.random.fold_in(seeds[5], 71), 0),
        "list_two": draw_list_two(jax.random.fold_in(seeds[5], 71), 0),
    }


LOG_FOUR = math.log(4.0)

def pooled(source, factor):
    stacked, grid_rows, grid_cols, channels = source.shape
    blocks = source.astype(jnp.float32).reshape(stacked, grid_rows // factor, factor, grid_cols // factor, factor, channels)
    return lax.optimization_barrier(jnp.mean(blocks, axis=(2, 4))).astype(jnp.bfloat16)

def far_blocks(coarse_grid, entries, block_cols, row_anchor, col_anchor):
    channels = coarse_grid.shape[-1]
    usable = entries >= 0
    clamped = jnp.maximum(entries, 0)
    top_rows = (clamped // block_cols * 8 - row_anchor).astype(jnp.int32)
    left_cols = (clamped % block_cols * 8 - col_anchor).astype(jnp.int32)

    def pick_block(start_row, start_col):
        anchor_zero = jnp.zeros((), jnp.int32)
        return lax.dynamic_slice(coarse_grid, (anchor_zero, start_row, start_col, anchor_zero), (2, 8, 8, channels))
    gathered = jax.vmap(pick_block)(top_rows, left_cols)
    slot_count = entries.shape[0]
    key_value = jnp.moveaxis(gathered, 1, 0).reshape(2, slot_count * 64, channels)
    return (key_value, jnp.repeat(usable, 64))

def contract(form, left, right):
    return jnp.einsum(form, left.astype(jnp.float32), right.astype(jnp.float32))

def attend(tile_q, window, inside, far_sets):
    tile_rows, tile_cols, channels = tile_q.shape
    head_dim = channels // HEADS
    pairs = HEADS // 2
    score_scale = 1.0 / math.sqrt(head_dim)
    across = tile_cols // 8
    count = tile_rows // 8 * across
    query_blocks = jnp.transpose(tile_q.reshape(tile_rows // 8, 8, across, 8, channels), (0, 2, 1, 3, 4))
    query_pairs = jnp.transpose(query_blocks.reshape(count * 64, pairs, 2 * head_dim), (1, 0, 2))
    near_list = []
    ok_list = []
    for index in range(count):
        block_row = index // across
        block_col = index % across
        near_list.append(window[:, 8 * block_row:8 * block_row + 24, 8 * block_col:8 * block_col + 24].reshape(2, 576, channels))
        ok_list.append(inside[8 * block_row:8 * block_row + 24, 8 * block_col:8 * block_col + 24].reshape(576))
    near_all = jnp.stack(near_list, axis=1).reshape(2, count, 576, pairs, 2 * head_dim)
    near_pairs = jnp.transpose(near_all, (3, 0, 1, 2, 4))
    near_ok = jnp.stack(ok_list)
    far_all = jnp.concatenate([pair_kv for pair_kv, usable in far_sets], axis=1)
    far_len = far_all.shape[1]
    far_pairs = jnp.transpose(far_all.reshape(2, far_len, pairs, 2 * head_dim), (2, 0, 1, 3))
    bias_list = []
    for depth in range(len(far_sets)):
        bias_list.append(jnp.where(far_sets[depth][1], (depth + 1) * LOG_FOUR, -1e+30).astype(jnp.float32))
    far_bias = jnp.concatenate(bias_list)

    def one_pair(items):
        query_part, near_part, far_part = items
        query_heads = query_part.reshape(count, 64, 2, head_dim)
        near_keys = near_part[0].reshape(count, 576, 2, head_dim)
        near_values = near_part[1].reshape(count, 576, 2, head_dim)
        far_keys = far_part[0].reshape(far_len, 2, head_dim)
        far_values = far_part[1].reshape(far_len, 2, head_dim)
        near_scores = jnp.where(near_ok[:, None, None, :], contract('bqhd,bkhd->bhqk', query_heads, near_keys) * score_scale, -1e+30)
        far_scores = contract('bqhd,khd->bhqk', query_heads, far_keys) * score_scale + far_bias
        highest = jnp.maximum(lax.optimization_barrier(jnp.max(near_scores, axis=3)), lax.optimization_barrier(jnp.max(far_scores, axis=3)))[:, :, :, None]
        near_weights = jnp.exp(near_scores - highest)
        far_weights = jnp.exp(far_scores - highest)
        totals = lax.optimization_barrier(jnp.sum(near_weights, axis=3)) + lax.optimization_barrier(jnp.sum(far_weights, axis=3))
        merged = contract('bhqk,bkhd->bqhd', near_weights.astype(jnp.bfloat16), near_values)
        merged = merged + contract('bhqk,khd->bqhd', far_weights.astype(jnp.bfloat16), far_values)
        merged = merged / jnp.transpose(totals, (0, 2, 1))[:, :, :, None]
        return merged.reshape(count * 64, 2 * head_dim)
    outputs = lax.map(one_pair, (query_pairs, near_pairs, far_pairs))
    outputs = jnp.transpose(outputs, (1, 0, 2)).reshape(tile_rows // 8, across, 8, 8, channels)
    return jnp.transpose(outputs, (0, 2, 1, 3, 4)).reshape(tile_rows, tile_cols, channels).astype(jnp.bfloat16)

def reference(queries, keys, values, list_one, list_two):
    image_rows, image_cols, channels = queries.shape
    key_value = jnp.stack([keys, values])
    padded = jnp.pad(key_value, ((0, 0), (8, 8), (8, 8), (0, 0)))
    inside_all = jnp.pad(jnp.ones((image_rows, image_cols), jnp.int32), 8) > 0
    levels = [(pooled(key_value, 2), list_one, 16), (pooled(key_value, 4), list_two, 32)]
    group_cols = image_cols // TILE

    def one_group(group_index):
        top_row = group_index // group_cols * TILE
        left_col = group_index % group_cols * TILE
        anchor_zero = jnp.zeros((), jnp.int32)
        tile_q = lax.dynamic_slice(queries, (top_row, left_col, anchor_zero), (TILE, TILE, channels))
        window = lax.dynamic_slice(padded, (anchor_zero, top_row, left_col, anchor_zero), (2, TILE + 16, TILE + 16, channels))
        inside = lax.dynamic_slice(inside_all, (top_row, left_col), (TILE + 16, TILE + 16))
        far_sets = []
        for coarse_grid, table, span in levels:
            block_cols = image_cols // span
            block_id = top_row // span * block_cols + left_col // span
            far_sets.append(far_blocks(coarse_grid, table[block_id], block_cols, 0, 0))
        return attend(tile_q, window, inside, far_sets)
    group_count = image_rows // TILE * (image_cols // TILE)
    groups = lax.map(one_group, jnp.arange(group_count, dtype=jnp.int32))
    groups = groups.reshape(image_rows // TILE, image_cols // TILE, TILE, TILE, channels)
    return jnp.transpose(groups, (0, 2, 1, 3, 4)).reshape(image_rows, image_cols, channels)
```

```python
import math

import jax
import jax.numpy as jnp
import numpy as np
from jax import lax
from jax.experimental import pallas as pl
from jax.experimental.pallas import tpu as pltpu
from jax.sharding import Mesh, PartitionSpec as P

BF = jnp.bfloat16
F32 = jnp.float32
NEG = -1e30
VMEM = pl.BlockSpec(memory_space=pltpu.VMEM)
SMEM = pl.BlockSpec(memory_space=pltpu.SMEM)


def split_bias(level):
    full = 2.0 * level * math.log(2.0)
    high = float(np.float32(full).astype(BF))
    return high, float(np.float32(full - high).astype(BF))


def iota(shape, dim):
    return lax.broadcasted_iota(jnp.int32, shape, dim)


def prep_kernel(q_ref, k_ref, v_ref, coarse_ref, fine_ref):
    row = iota((80, 256), 0)
    tok = iota((80, 256), 1)
    trow, tcol = tok >> 4, tok & 15
    one = (row < 64) & ((trow >> 1) == (row >> 3)) & ((tcol >> 1) == (row & 7))
    rest = row - 64
    two = (row >= 64) & ((trow >> 2) == (rest >> 2)) & ((tcol >> 2) == (rest & 3))
    pool = jnp.where(one, 0.25, jnp.where(two, 0.0625, 0.0)).astype(BF)
    k = k_ref[...]
    v = v_ref[...]
    kc = jnp.dot(pool, k, preferred_element_type=F32).astype(BF)
    vc = jnp.dot(pool, v, preferred_element_type=F32).astype(BF)
    q = (q_ref[...].astype(F32) * 0.125).astype(BF)
    for j in range(4):
        pair = slice(128 * j, 128 * j + 128)
        third = slice(512 + 64 * j, 576 + 64 * j)
        fine_ref[j, 0:256, 0:128] = k[:, pair]
        fine_ref[j, 0:256, 128:256] = v[:, pair]
        fine_ref[j, 0:256, 256:384] = jnp.concatenate([k[:, third], v[:, third]], axis=1)
        fine_ref[j, 256:384, 0:128] = q[0:128, pair]
        fine_ref[j, 256:384, 128:256] = q[128:256, pair]
        fine_ref[j, 256:384, 256:384] = jnp.concatenate(
            [q[0:128, third], q[128:256, third]], axis=1
        )
        both = jnp.concatenate([kc[:, third], vc[:, third]], axis=1)
        for core in range(2):
            coarse_ref[j, core, :, 0:128] = kc[:, pair]
            coarse_ref[j, core, :, 128:256] = vc[:, pair]
            coarse_ref[j, core, :, 256:384] = both


def unpack_kernel(o_ref, out_ref):
    for j in range(4):
        pair = slice(128 * j, 128 * j + 128)
        out_ref[0:128, pair] = o_ref[j, :, 0:128]
        out_ref[128:256, pair] = o_ref[j, :, 128:256]
    lane = iota((128, 128), 1)
    for j in (0, 2):
        first = o_ref[j, :, 256:384]
        second = o_ref[j + 1, :, 256:384]
        lanes = slice(512 + 64 * j, 640 + 64 * j)
        out_ref[0:128, lanes] = jnp.concatenate([first[:, :64], second[:, :64]], axis=1)
        out_ref[128:256, lanes] = jnp.concatenate([first[:, 64:], second[:, 64:]], axis=1)


NEAR = 1024
FAR = 27 * 64
KEYS = NEAR + 2 * FAR


def attend_kernel(
    place_ref, idx_one_ref, idx_two_ref,
    own_ref, inner_ref, outer_ref, q_ref, rc_ref, side_ref, ys_ref,
    out_ref, one_ref, two_ref, kv_ref, s_ref, p_ref,
):
    y = place_ref[0]
    z = place_ref[1]
    core = place_ref[2]

    def quarter(xs, kk):
        return slice(32 * (xs & 1) + 16 * kk, 32 * (xs & 1) + 16 * kk + 16)

    for xs in range(4):
        for kk in range(2):
            one_ref[(2 + xs) * 6 + 2 + kk] = rc_ref[xs, kk, 0:64]
            two_ref[(3 + xs // 2) * 7 + 3, quarter(xs, kk)] = rc_ref[xs, kk, 64:80]
    for s in range(2):
        for xs in range(4):
            for kk in range(2):
                base = (2 * xs + kk) * 80
                one_ref[(2 + xs) * 6 + 4 * s + kk] = side_ref[s, base:base + 64]
                col = 2 if s == 0 else 4
                two_ref[(3 + xs // 2) * 7 + col, quarter(xs, kk)] = side_ref[s, base + 64:base + 80]
                for far in (2, 3):
                    at = 640 + 128 * (far - 2) + (2 * xs + kk) * 16
                    col = 3 - far if s == 0 else 3 + far
                    two_ref[(3 + xs // 2) * 7 + col, quarter(xs, kk)] = side_ref[s, at:at + 16]
        for d in range(2):
            at0 = 832 * d
            for i in range(2):
                one_ref[(6 * d + i) * 6 + 2 + s] = ys_ref[s, at0 + 64 * i:at0 + 64 * i + 64]
                for kk in range(2):
                    at = at0 + 128 + (2 * i + kk) * 64
                    one_ref[(6 * d + i) * 6 + 4 * s + kk] = ys_ref[s, at:at + 64]
            brow = 1 + 4 * d
            for xs in range(4):
                at = at0 + 384 + xs * 16
                two_ref[(brow + xs // 2) * 7 + 3, quarter(xs, s)] = ys_ref[s, at:at + 16]
                for far in (1, 2, 3):
                    col = 3 - far if s == 0 else 3 + far
                    for kk in range(2):
                        at = at0 + 448 + 128 * (far - 1) + (2 * xs + kk) * 16
                        two_ref[(brow + xs // 2) * 7 + col, quarter(xs, kk)] = ys_ref[s, at:at + 16]
        brow = jnp.where(y >= 2, 0, 7)
        for i in range(2):
            at = 1664 + 16 * i
            two_ref[brow * 7 + 3, quarter(i, s)] = ys_ref[s, at:at + 16]
            for far in (1, 2, 3):
                col = 3 - far if s == 0 else 3 + far
                for kk in range(2):
                    at = 1664 + 32 + 64 * (far - 1) + (2 * i + kk) * 16
                    two_ref[brow * 7 + col, quarter(i, kk)] = ys_ref[s, at:at + 16]

    lane64 = iota((64, 128), 1)
    high_one, low_one = split_bias(1)
    high_two, low_two = split_bias(2)
    tok = iota((256, 128), 0)
    lane = iota((256, 128), 1)
    block = ((tok >> 7) << 1) + ((tok >> 3) & 1)
    q_feat = jnp.where((lane == block) | (lane == 4) | (lane == 5), 1.0, 0.0).astype(BF)

    def near_features(rows_wide, wide_log, col_base, tile):
        count = rows_wide << wide_log
        key = iota((count, 128), 0)
        ln = iota((count, 128), 1)
        wr = key >> wide_log
        wc = (key & ((1 << wide_log) - 1)) + col_base
        br, bc = ln >> 1, ln & 1
        row = 64 * y + 16 * tile - 8 + wr
        col = 32 * z + 16 * core - 8 + wc
        ok = (wr >= 8 * br) & (wr < 8 * br + 24) & (wc >= 8 * bc) & (wc < 8 * bc + 24)
        ok = ok & (row >= 0) & (row < 256) & (col >= 0) & (col < 256)
        return jnp.where((ln < 4) & jnp.logical_not(ok), NEG, 0.0).astype(BF)

    def place_rows(at, size, packed, features):
        kv_ref[at:at + size, 0:128] = packed[:, 0:128]
        kv_ref[at:at + size, 128:256] = features
        kv_ref[at:at + size, 256:384] = packed[:, 256:384]
        kv_ref[at:at + size, 384:512] = packed[:, 128:256]

    def one_tile(tile, carry):
        at = pl.multiple_of(tile * 256, 256)
        place_rows(0, 512, own_ref[pl.ds(at, 512)], near_features(32, 4, 8, tile))
        at = pl.multiple_of(tile * 128, 128)
        inner_col = 24 - 24 * core
        place_rows(512, 256, inner_ref[pl.ds(at, 256)], near_features(32, 3, inner_col, tile))
        place_rows(768, 256, outer_ref[pl.ds(at, 256)], near_features(32, 3, 24 - inner_col, tile))

        def far_block(j, c):
            for level, (idx_ref, win_ref, trow, high, low) in enumerate((
                (idx_one_ref, one_ref, tile, high_one, low_one),
                (idx_two_ref, two_ref, tile // 2, high_two, low_two),
            )):
                index = idx_ref[trow, j]
                packed = win_ref[jnp.maximum(index, 0)]
                top = jnp.where(index >= 0, jnp.float32(high), jnp.float32(NEG))
                feat = jnp.where(lane64 == 4, top, jnp.where(lane64 == 5, low, 0.0)).astype(BF)
                start = pl.multiple_of(NEAR + level * FAR + j * 64, 64)
                kv_ref[pl.ds(start, 64), 0:128] = packed[:, 0:128]
                kv_ref[pl.ds(start, 64), 128:256] = feat
                kv_ref[pl.ds(start, 64), 256:384] = packed[:, 256:384]
                kv_ref[pl.ds(start, 64), 384:512] = packed[:, 128:256]
            return c

        lax.fori_loop(0, 27, far_block, 0)

        q_pair = jnp.concatenate([q_ref[tile, 0:128, 0:128], q_ref[tile, 0:128, 128:256]], axis=0)
        q_last = q_ref[tile, 0:128, 256:384]
        q_third = jnp.concatenate([q_last, jnp.concatenate([q_last[:, 64:], q_last[:, :64]], axis=1)], axis=0)
        zero = jnp.zeros_like(q_pair)
        low_half = lane < 64
        outs = []
        for head in range(3):
            if head < 2:
                keep = low_half if head == 0 else jnp.logical_not(low_half)
                lhs = jnp.concatenate([jnp.where(keep, q_pair, zero), q_feat], axis=1)
                k_lanes, v_lanes = slice(0, 256), slice(384, 512)
            else:
                lhs = jnp.concatenate([q_feat, jnp.where(low_half, q_third, zero)], axis=1)
                k_lanes, v_lanes = slice(128, 384), slice(256, 384)
            s_ref[...] = lax.dot_general(
                lhs, kv_ref[:, k_lanes], (((1,), (1,)), ((), ())), preferred_element_type=F32
            )
            top = jnp.max(s_ref[...], axis=1, keepdims=True)
            weights = jnp.exp(s_ref[...] - top)
            total = jnp.sum(weights, axis=1, keepdims=True)
            p_ref[...] = weights.astype(BF)
            acc = jnp.dot(p_ref[...], kv_ref[:, v_lanes], preferred_element_type=F32)
            outs.append(acc / total)
        pair_out = jnp.where(low_half, outs[0], outs[1])
        third_out = outs[2]
        out_ref[tile, :, 0:128] = pair_out[0:128].astype(BF)
        out_ref[tile, :, 128:256] = pair_out[128:256].astype(BF)
        out_ref[tile, :, 256:384] = jnp.concatenate(
            [third_out[0:128, 64:], third_out[128:256, 64:]], axis=1
        ).astype(BF)
        return carry

    lax.fori_loop(0, 4, one_tile, 0)


def call(kernel, out_shape, in_specs, scratch=(), flops=0, nbytes=0):
    return pl.pallas_call(
        kernel,
        out_shape=out_shape,
        in_specs=in_specs,
        out_specs=jax.tree.map(lambda _: VMEM, out_shape),
        scratch_shapes=scratch,
        compiler_params=pltpu.CompilerParams(vmem_limit_bytes=56 * 2**20),
        cost_estimate=pl.CostEstimate(flops=flops, bytes_accessed=nbytes, transcendentals=0),
    )


def shape(*dims):
    return jax.ShapeDtypeStruct(dims, BF)


def z_perm(step):
    pairs = []
    for z in range(8):
        if z + step < 8:
            pairs.append((2 * z + 1, 2 * (z + step)))
        if z - step >= 0:
            pairs.append((2 * z, 2 * (z - step) + 1))
    return pairs


def body(queries, keys, values, list_one, list_two):
    y = lax.axis_index("y")
    x = lax.axis_index("x")
    z = lax.axis_index("z")
    core = lax.axis_index("core")
    up = [(i, i + 1) for i in range(3)]
    down = [(i + 1, i) for i in range(3)]
    across = [(i, i ^ 2) for i in range(4)]

    coarse, fine = call(
        prep_kernel, [shape(4, 2, 80, 384), shape(4, 384, 384)], [VMEM] * 3, nbytes=4 << 20
    )(queries.reshape(256, 768), keys.reshape(256, 768), values.reshape(256, 768))

    rc = lax.all_to_all(coarse.reshape(8, 80, 384), ("x", "core"), 0, 0, tiled=True)
    rc = rc.reshape(4, 2, 80, 384)

    z_one = lax.ppermute(rc, ("z", "core"), z_perm(1))
    last = rc[:, :, 64:80]
    z_two = lax.ppermute(last, ("z", "core"), z_perm(2))
    z_three = lax.ppermute(last, ("z", "core"), z_perm(3))

    rf = lax.all_to_all(fine, "x", 0, 0, tiled=True)
    tokens = rf[:, 0:256].reshape(64, 16, 384)
    top = lax.ppermute(tokens[56:64], "y", up)
    bottom = lax.ppermute(tokens[0:8], "y", down)
    tall = jnp.concatenate([top, tokens, bottom], axis=0)
    left, right = tall[:, 0:8], tall[:, 8:16]
    inner = lax.ppermute(jnp.where(core == 0, right, left).reshape(640, 384), "core", [(0, 1), (1, 0)])
    outer = lax.ppermute(jnp.where(core == 0, left, right).reshape(640, 384), ("z", "core"), z_perm(1))

    mine = lax.dynamic_index_in_dim(rc, core, 1, keepdims=False)

    def y_part(rows):
        return jnp.concatenate(
            [
                mine[rows, 0:64].reshape(128, 384),
                z_one[rows, :, 0:64].reshape(256, 384),
                mine[:, 64:80].reshape(64, 384),
                z_one[:, :, 64:80].reshape(128, 384),
                z_two.reshape(128, 384),
                z_three.reshape(128, 384),
            ],
            axis=0,
        )

    from_up = lax.ppermute(y_part(slice(2, 4)), "y", up)
    from_down = lax.ppermute(y_part(slice(0, 2)), "y", down)
    half = jnp.where(y < 2, 2, 0)

    def picked(array):
        return lax.dynamic_slice_in_dim(array, half, 2, axis=0)

    from_across = lax.ppermute(
        jnp.concatenate(
            [
                picked(mine)[:, 64:80].reshape(32, 384),
                picked(z_one)[:, :, 64:80].reshape(64, 384),
                picked(z_two).reshape(64, 384),
                picked(z_three).reshape(64, 384),
            ],
            axis=0,
        ),
        "y",
        across,
    )

    side = lax.all_gather(
        jnp.concatenate(
            [z_one.reshape(640, 384), z_two.reshape(128, 384), z_three.reshape(128, 384)], axis=0
        ),
        "core",
    )
    ys = lax.all_gather(jnp.concatenate([from_up, from_down, from_across], axis=0), "core")

    rows_one = 4 * y + jnp.arange(4, dtype=jnp.int32)
    entries = list_one[rows_one * 16 + 2 * z + core]
    place = (entries // 16 - (4 * y - 2)) * 6 + entries % 16 - (2 * z - 2)
    idx_one = jnp.where(entries >= 0, place, -1)
    rows_two = 2 * y + jnp.arange(2, dtype=jnp.int32)
    entries = list_two[rows_two * 8 + z]
    place = (entries // 8 - (2 * y - 3)) * 7 + entries % 8 - (z - 3)
    idx_two = jnp.where(entries >= 0, place, -1)

    out = call(
        attend_kernel,
        shape(4, 128, 384),
        [SMEM] * 3 + [VMEM] * 7,
        scratch=[
            pltpu.VMEM((48, 64, 384), BF),
            pltpu.VMEM((56, 64, 384), BF),
            pltpu.VMEM((KEYS, 512), BF),
            pltpu.VMEM((256, KEYS), F32),
            pltpu.VMEM((256, KEYS), BF),
        ],
        flops=12 * 256 * KEYS * 768,
        nbytes=10 << 20,
    )(
        jnp.stack([y, z, core]).astype(jnp.int32), idx_one, idx_two,
        tall.reshape(1280, 384), inner, outer, rf[:, 256:384], rc, side, ys,
    )
    back = lax.all_to_all(out, "x", 0, 0, tiled=True)
    tile = call(unpack_kernel, shape(256, 768), [VMEM], nbytes=1 << 20)(back)
    return tile.reshape(16, 16, 768)


def solution(mesh):
    fine_mesh = Mesh(mesh.devices.reshape(4, 4, 8, 2), ("y", "x", "z", "core"))
    spec = P(("y", "x"), ("z", "core"), None)
    return jax.shard_map(
        body, mesh=fine_mesh, in_specs=(spec, spec, spec, P(), P()), out_specs=spec, check_vma=False
    )
```

```python
import math

import jax
import jax.numpy as jnp
import numpy as np
from jax import lax
from jax.experimental import pallas as pl
from jax.experimental.pallas import tpu as pltpu
from jax.sharding import Mesh, PartitionSpec as P

BF = jnp.bfloat16
F32 = jnp.float32
NEG = -1e30
VMEM = pl.BlockSpec(memory_space=pltpu.VMEM)
SMEM = pl.BlockSpec(memory_space=pltpu.SMEM)


def split_bias(level):
    full = 2.0 * level * math.log(2.0)
    high = float(np.float32(full).astype(BF))
    return high, float(np.float32(full - high).astype(BF))


def iota(shape, dim):
    return lax.broadcasted_iota(jnp.int32, shape, dim)


FINE, QUERY, ONE, TWO, PACKED = 0, 256, 384, 448, 464


def prep_kernel(q_ref, k_ref, v_ref, out_ref):
    row = iota((80, 256), 0)
    tok = iota((80, 256), 1)
    trow, tcol = tok >> 4, tok & 15
    one = (row < 64) & ((trow >> 1) == (row >> 3)) & ((tcol >> 1) == (row & 7))
    rest = row - 64
    two = (row >= 64) & ((trow >> 2) == (rest >> 2)) & ((tcol >> 2) == (rest & 3))
    pool = jnp.where(one, 0.25, jnp.where(two, 0.0625, 0.0)).astype(BF)
    k = k_ref[...]
    v = v_ref[...]
    kc = jnp.dot(pool, k, preferred_element_type=F32).astype(BF)
    vc = jnp.dot(pool, v, preferred_element_type=F32).astype(BF)
    q = (q_ref[...].astype(F32) * 0.125).astype(BF)
    for j in range(4):
        pair = slice(128 * j, 128 * j + 128)
        third = slice(512 + 64 * j, 576 + 64 * j)
        out_ref[j, FINE:QUERY, 0:128] = k[:, pair]
        out_ref[j, FINE:QUERY, 128:256] = v[:, pair]
        out_ref[j, FINE:QUERY, 256:384] = jnp.concatenate([k[:, third], v[:, third]], axis=1)
        out_ref[j, QUERY:ONE, 0:128] = q[0:128, pair]
        out_ref[j, QUERY:ONE, 128:256] = q[128:256, pair]
        out_ref[j, QUERY:ONE, 256:384] = jnp.concatenate(
            [q[0:128, third], q[128:256, third]], axis=1
        )
        out_ref[j, ONE:PACKED, 0:128] = kc[:, pair]
        out_ref[j, ONE:PACKED, 128:256] = vc[:, pair]
        out_ref[j, ONE:PACKED, 256:384] = jnp.concatenate([kc[:, third], vc[:, third]], axis=1)


def unpack_kernel(o_ref, out_ref):
    for j in range(4):
        pair = slice(128 * j, 128 * j + 128)
        out_ref[0:128, pair] = o_ref[j, :, 0:128]
        out_ref[128:256, pair] = o_ref[j, :, 128:256]
    lane = iota((128, 128), 1)
    for j in (0, 2):
        first = o_ref[j, :, 256:384]
        second = o_ref[j + 1, :, 256:384]
        lanes = slice(512 + 64 * j, 640 + 64 * j)
        out_ref[0:128, lanes] = jnp.concatenate([first[:, :64], second[:, :64]], axis=1)
        out_ref[128:256, lanes] = jnp.concatenate([first[:, 64:], second[:, 64:]], axis=1)


NEAR = 1024
FAR = 27 * 64
KEYS = NEAR + 2 * FAR


CHUNKS = [(at, min(512, KEYS - at)) for at in range(0, KEYS, 512)]


def attend_kernel(
    place_ref, idx_one_ref, idx_two_ref,
    own_ref, other_ref, up_ref, down_ref, inner_ref, side_ref, other_side_ref,
    row_ref, up_two_ref, down_two_ref, across_ref,
    other_row_ref, other_up_ref, other_down_ref, other_across_ref,
    out_ref, one_ref, two_ref, tall_ref, kv_ref, s_ref,
):
    y = place_ref[0]
    z = place_ref[1]
    core = place_ref[2]

    tall_ref[0:128] = up_ref[256:384]
    tall_ref[1152:1280] = down_ref[256:384]
    for xs in range(4):
        tall_ref[128 + 256 * xs:384 + 256 * xs] = own_ref[xs, FINE:QUERY]

    def quarter(xs, kk):
        return pl.ds(pl.multiple_of(32 * (xs & 1) + 16 * kk, 16), 16)

    def put_one(row, col, block):
        one_ref[row * 6 + col] = block

    for m in range(2):
        kk = core if m == 0 else 1 - core
        mine = own_ref if m == 0 else other_ref
        base = ONE if m == 0 else 0
        for xs in range(4):
            put_one(2 + xs, 2 + kk, mine[xs, base:base + 64])
        for i in range(2):
            at = 128 * m + 64 * i
            put_one(i, 2 + kk, up_ref[at:at + 64])
            put_one(6 + i, 2 + kk, down_ref[at:at + 64])
    for side, one_side in ((core, side_ref), (1 - core, other_side_ref)):
        for m in range(2):
            kk = 1 - side if m == 0 else side
            for i in range(4):
                at = 256 * m + 64 * i
                put_one(2 + i, 4 * side + kk, one_side[at:at + 64])
            for i in range(2):
                at = 512 + 128 * m + 64 * i
                put_one(i, 4 * side + kk, one_side[at:at + 64])
                put_one(6 + i, 4 * side + kk, one_side[at + 256:at + 320])
    end = jnp.where(y >= 2, 2 * y - 1, 2 * y + 6)
    for kk, row, ups, downs, across in (
        (core, row_ref, up_two_ref, down_two_ref, across_ref),
        (1 - core, other_row_ref, other_up_ref, other_down_ref, other_across_ref),
    ):
        for col in range(8):
            for xs in range(4):
                at = 64 * col + 16 * xs
                brow = 2 * y + 2 + xs // 2
                two_ref[brow * 8 + col, quarter(xs, kk)] = row[at:at + 16]
                two_ref[(brow - 2) * 8 + col, quarter(xs, kk)] = ups[at:at + 16]
                two_ref[(brow + 2) * 8 + col, quarter(xs, kk)] = downs[at:at + 16]
            for i in range(2):
                at = 32 * col + 16 * i
                two_ref[end * 8 + col, quarter(i, kk)] = across[at:at + 16]

    lane64 = iota((64, 128), 1)
    high_one, low_one = split_bias(1)
    high_two, low_two = split_bias(2)
    tok = iota((256, 128), 0)
    lane = iota((256, 128), 1)
    block = ((tok >> 7) << 1) + ((tok >> 3) & 1)
    q_feat = jnp.where((lane == block) | (lane == 4) | (lane == 5), 1.0, 0.0).astype(BF)

    def near_features(rows_wide, wide_log, col_base, tile):
        count = rows_wide << wide_log
        key = iota((count, 128), 0)
        ln = iota((count, 128), 1)
        wr = key >> wide_log
        wc = (key & ((1 << wide_log) - 1)) + col_base
        br, bc = ln >> 1, ln & 1
        row = 64 * y + 16 * tile - 8 + wr
        col = 32 * z + 16 * core - 8 + wc
        ok = (wr >= 8 * br) & (wr < 8 * br + 24) & (wc >= 8 * bc) & (wc < 8 * bc + 24)
        ok = ok & (row >= 0) & (row < 256) & (col >= 0) & (col < 256)
        return jnp.where(
            (ln < 4) & jnp.logical_not(ok), NEG, jnp.where(ln == 6, 1.0, 0.0)
        ).astype(BF)

    def place_rows(at, size, packed, features):
        kv_ref[pl.ds(at, size), 0:128] = packed[:, 0:128]
        kv_ref[pl.ds(at, size), 128:256] = features
        kv_ref[pl.ds(at, size), 256:384] = packed[:, 256:384]
        kv_ref[pl.ds(at, size), 384:512] = packed[:, 128:256]

    def one_tile(tile, carry):
        at = pl.multiple_of(tile * 256, 256)
        place_rows(0, 512, tall_ref[pl.ds(at, 512)], near_features(32, 4, 8, tile))
        at = pl.multiple_of(tile * 128, 128)
        inner_col = 24 - 24 * core
        place_rows(512, 256, inner_ref[pl.ds(at, 256)], near_features(32, 3, inner_col, tile))
        place_rows(768, 256, side_ref[pl.ds(pl.multiple_of(1024 + tile * 128, 128), 256)], near_features(32, 3, 24 - inner_col, tile))

        def far_block(j, c):
            for level, (idx_ref, win_ref, trow, high, low) in enumerate((
                (idx_one_ref, one_ref, tile, high_one, low_one),
                (idx_two_ref, two_ref, tile // 2, high_two, low_two),
            )):
                index = idx_ref[trow, j]
                top = jnp.where(index >= 0, jnp.float32(high), jnp.float32(NEG))
                feat = jnp.where(
                    lane64 == 4, top, jnp.where(lane64 == 5, low, jnp.where(lane64 == 6, 1.0, 0.0))
                )
                start = pl.multiple_of(NEAR + level * FAR + j * 64, 64)
                place_rows(start, 64, win_ref[jnp.where(index >= 0, index, -1 - index)], feat.astype(BF))
            return c

        lax.fori_loop(0, 27, far_block, 0)

        q_pair = jnp.concatenate([own_ref[tile, QUERY:ONE, 0:128], own_ref[tile, QUERY:ONE, 128:256]], axis=0)
        q_last = own_ref[tile, QUERY:ONE, 256:384]
        q_third = jnp.concatenate([q_last, jnp.concatenate([q_last[:, 64:], q_last[:, :64]], axis=1)], axis=0)
        zero = jnp.zeros_like(q_pair)
        low_half = lane < 64
        lhs = [
            jnp.concatenate([jnp.where(low_half, q_pair, zero), q_feat], axis=1),
            jnp.concatenate([jnp.where(low_half, zero, q_pair), q_feat], axis=1),
            jnp.concatenate([q_feat, jnp.where(low_half, q_third, zero)], axis=1),
        ]

        def scores(head, at, size, top):
            lanes = slice(128, 384) if head == 2 else slice(0, 256)
            s = lax.dot_general(
                lhs[head], kv_ref[at:at + size, lanes], (((1,), (1,)), ((), ())),
                preferred_element_type=F32,
            )
            s_ref[head % 2, :, at:at + size] = s
            for c in range(0, size, 128):
                part = s[:, c:c + 128]
                top = part if top is None else jnp.maximum(top, part)
            return top

        def values(head, at, size, peak, acc):
            w = jnp.exp(s_ref[head % 2, :, at:at + size] - peak).astype(BF)
            if head == 2:
                rhs = kv_ref[at:at + size, 128:384]
            else:
                rhs = jnp.concatenate(
                    [kv_ref[at:at + size, 128:256], kv_ref[at:at + size, 384:512]], axis=1
                )
            part = jnp.dot(w, rhs, preferred_element_type=F32)
            return part if acc is None else acc + part

        top = None
        for at, size in CHUNKS:
            top = scores(0, at, size, top)
        outs = []
        for head in range(3):
            peak = jnp.max(top, axis=1, keepdims=True)
            top = acc = None
            for at, size in CHUNKS:
                if head < 2:
                    top = scores(head + 1, at, size, top)
                acc = values(head, at, size, peak, acc)
            outs.append(acc[:, 128:256] / acc[:, 6:7])
        pair_out = jnp.where(low_half, outs[0], outs[1])
        third_out = outs[2]
        out_ref[tile, :, 0:128] = pair_out[0:128].astype(BF)
        out_ref[tile, :, 128:256] = pair_out[128:256].astype(BF)
        out_ref[tile, :, 256:384] = jnp.concatenate(
            [third_out[0:128, 64:], third_out[128:256, 64:]], axis=1
        ).astype(BF)
        return carry

    lax.fori_loop(0, 4, one_tile, 0)


def call(kernel, out_shape, in_specs, scratch=(), flops=0, nbytes=0):
    return pl.pallas_call(
        kernel,
        out_shape=out_shape,
        in_specs=in_specs,
        out_specs=jax.tree.map(lambda _: VMEM, out_shape),
        scratch_shapes=scratch,
        compiler_params=pltpu.CompilerParams(vmem_limit_bytes=56 * 2**20),
        cost_estimate=pl.CostEstimate(flops=flops, bytes_accessed=nbytes, transcendentals=0),
    )


def shape(*dims):
    return jax.ShapeDtypeStruct(dims, BF)


def z_perm(step):
    pairs = []
    for z in range(8):
        if z + step < 8:
            pairs.append((2 * z + 1, 2 * (z + step)))
        if z - step >= 0:
            pairs.append((2 * z, 2 * (z - step) + 1))
    return pairs


def body(queries, keys, values, list_one, list_two):
    y = lax.axis_index("y")
    x = lax.axis_index("x")
    z = lax.axis_index("z")
    core = lax.axis_index("core")
    up = [(i, i + 1) for i in range(3)]
    down = [(i + 1, i) for i in range(3)]
    across = [(i, i ^ 2) for i in range(4)]

    entries = lax.dynamic_slice(list_one.reshape(16, 16, 27), (4 * y, 2 * z + core, 0), (4, 1, 27))[:, 0]
    where = (entries // 16 - (4 * y - 2)) * 6 + entries % 16 - (2 * z - 2)
    self_one = (2 + jnp.arange(4, dtype=jnp.int32)[:, None]) * 6 + 2 + core
    idx_one = jnp.where(entries >= 0, where, -1 - self_one)
    entries = lax.dynamic_slice(list_two.reshape(8, 8, 27), (2 * y, z, 0), (2, 1, 27))[:, 0]
    self_two = (2 * y + 2 + jnp.arange(2, dtype=jnp.int32)[:, None]) * 8 + z
    idx_two = jnp.where(entries >= 0, entries + 16, -1 - self_two)
    place = jnp.stack([y, z, core]).astype(jnp.int32)

    packed = call(prep_kernel, shape(4, PACKED, 384), [VMEM] * 3, nbytes=4 << 20)(
        queries.reshape(256, 768), keys.reshape(256, 768), values.reshape(256, 768)
    )
    rf = lax.all_to_all(packed, "x", 0, 0, tiled=True)
    rf, idx_one, idx_two, place = lax.optimization_barrier((rf, idx_one, idx_two, place))

    def over_core(array):
        return lax.ppermute(array, "core", [(0, 1), (1, 0)])

    def over_z(array, step=1):
        return lax.ppermute(array, ("z", "core"), z_perm(step))

    def strips(tokens):
        rows = tokens.shape[0] // 16
        tokens = tokens.reshape(rows, 16, 384)
        left, right = tokens[:, 0:8], tokens[:, 8:16]
        inner = jnp.where(core == 0, right, left).reshape(rows * 8, 384)
        outer = jnp.where(core == 0, left, right).reshape(rows * 8, 384)
        return inner, outer

    fine = rf[:, FINE:QUERY].reshape(1024, 384)
    other = over_core(rf[:, ONE:TWO].reshape(256, 384)).reshape(4, 64, 384)
    ones = (rf[:, ONE:TWO], other)
    two = rf[:, TWO:PACKED].reshape(1, 64, 384)
    row_two = lax.all_to_all(jnp.broadcast_to(two, (8, 64, 384)), "z", 0, 0, tiled=True)
    from_up = lax.ppermute(
        jnp.concatenate([t[2:4].reshape(128, 384) for t in ones] + [fine[896:1024]], axis=0), "y", up
    )
    from_down = lax.ppermute(
        jnp.concatenate([t[0:2].reshape(128, 384) for t in ones] + [fine[0:128]], axis=0), "y", down
    )
    row_two, from_up, from_down = lax.optimization_barrier((row_two, from_up, from_down))

    top_inner, top_outer = strips(from_up[256:384])
    middle_inner, middle_outer = strips(fine)
    bottom_inner, bottom_outer = strips(from_down[256:384])
    side = over_z(
        jnp.concatenate(
            [t.reshape(256, 384) for t in ones]
            + [from_up[0:256], from_down[0:256], top_outer, middle_outer, bottom_outer],
            axis=0,
        )
    )
    inner = over_core(jnp.concatenate([top_inner, middle_inner, bottom_inner], axis=0))
    up_two = lax.ppermute(row_two.reshape(512, 384), "y", up)
    down_two = lax.ppermute(row_two.reshape(512, 384), "y", down)
    half = jnp.where(y < 2, 1, 0)
    across_two = lax.ppermute(
        lax.dynamic_index_in_dim(row_two.reshape(8, 2, 32, 384), half, 1, keepdims=False).reshape(256, 384),
        "y",
        across,
    )
    other_row = over_core(row_two.reshape(512, 384))
    side, up_two, down_two, across_two, inner, other_row = lax.optimization_barrier(
        (side, up_two, down_two, across_two, inner, other_row)
    )

    other_side = over_core(side[0:1024])
    others = [over_core(t) for t in (up_two, down_two, across_two)]

    out = call(
        attend_kernel,
        shape(4, 128, 384),
        [SMEM] * 3 + [VMEM] * 15,
        scratch=[
            pltpu.VMEM((48, 64, 384), BF),
            pltpu.VMEM((96, 64, 384), BF),
            pltpu.VMEM((1280, 384), BF),
            pltpu.VMEM((KEYS, 512), BF),
            pltpu.VMEM((2, 256, KEYS), F32),
        ],
        flops=12 * 256 * KEYS * 768,
        nbytes=10 << 20,
    )(
        place, idx_one, idx_two, rf, other, from_up, from_down, inner, side, other_side,
        row_two.reshape(512, 384), up_two, down_two, across_two, other_row, *others,
    )
    back = lax.all_to_all(out, "x", 0, 0, tiled=True)
    tile = call(unpack_kernel, shape(256, 768), [VMEM], nbytes=1 << 20)(back)
    return tile.reshape(16, 16, 768)


def solution(mesh):
    fine_mesh = Mesh(mesh.devices.reshape(4, 4, 8, 2), ("y", "x", "z", "core"))
    spec = P(("y", "x"), ("z", "core"), None)
    return jax.shard_map(
        body, mesh=fine_mesh, in_specs=(spec, spec, spec, P(), P()), out_specs=spec, check_vma=False
    )
```

```python
import math

import jax
import jax.numpy as jnp
import numpy as np
from jax import lax
from jax.experimental import pallas as pl
from jax.experimental.pallas import tpu as pltpu
from jax.sharding import Mesh, PartitionSpec as P

BF = jnp.bfloat16
F32 = jnp.float32
NEG = -1e30
VMEM = pl.BlockSpec(memory_space=pltpu.VMEM)
SMEM = pl.BlockSpec(memory_space=pltpu.SMEM)


def split_bias(level):
    full = 2.0 * level * math.log(2.0)
    high = float(np.float32(full).astype(BF))
    return high, float(np.float32(full - high).astype(BF))


def iota(shape, dim):
    return lax.broadcasted_iota(jnp.int32, shape, dim)


FINE, QUERY, ONE, PACKED = 0, 256, 384, 448


def prep_kernel(q_ref, k_ref, v_ref, two_ref, out_ref):
    row = iota((80, 256), 0)
    tok = iota((80, 256), 1)
    trow, tcol = tok >> 4, tok & 15
    one = (row < 64) & ((trow >> 1) == (row >> 3)) & ((tcol >> 1) == (row & 7))
    rest = row - 64
    two = (row >= 64) & ((trow >> 2) == (rest >> 2)) & ((tcol >> 2) == (rest & 3))
    pool = jnp.where(one, 0.25, jnp.where(two, 0.0625, 0.0)).astype(BF)
    k = k_ref[...]
    v = v_ref[...]
    kc = jnp.dot(pool, k, preferred_element_type=F32).astype(BF)
    vc = jnp.dot(pool, v, preferred_element_type=F32).astype(BF)
    q = (q_ref[...].astype(F32) * 0.125).astype(BF)
    for j in range(4):
        pair = slice(128 * j, 128 * j + 128)
        third = slice(512 + 64 * j, 576 + 64 * j)
        out_ref[j, FINE:QUERY, 0:128] = k[:, pair]
        out_ref[j, FINE:QUERY, 128:256] = v[:, pair]
        out_ref[j, FINE:QUERY, 256:384] = jnp.concatenate([k[:, third], v[:, third]], axis=1)
        out_ref[j, QUERY:ONE, 0:128] = q[0:128, pair]
        out_ref[j, QUERY:ONE, 128:256] = q[128:256, pair]
        out_ref[j, QUERY:ONE, 256:384] = jnp.concatenate(
            [q[0:128, third], q[128:256, third]], axis=1
        )
        both = jnp.concatenate([kc[:, third], vc[:, third]], axis=1)
        for lanes, part in ((0, kc[:, pair]), (128, vc[:, pair]), (256, both)):
            out_ref[j, ONE:PACKED, lanes:lanes + 128] = part[0:64]
            for core in range(2):
                two_ref[j, core, :, lanes:lanes + 128] = part[64:80]


def unpack_kernel(o_ref, out_ref):
    for j in range(4):
        pair = slice(128 * j, 128 * j + 128)
        out_ref[0:128, pair] = o_ref[j, :, 0:128]
        out_ref[128:256, pair] = o_ref[j, :, 128:256]
    lane = iota((128, 128), 1)
    for j in (0, 2):
        first = o_ref[j, :, 256:384]
        second = o_ref[j + 1, :, 256:384]
        lanes = slice(512 + 64 * j, 640 + 64 * j)
        out_ref[0:128, lanes] = jnp.concatenate([first[:, :64], second[:, :64]], axis=1)
        out_ref[128:256, lanes] = jnp.concatenate([first[:, 64:], second[:, 64:]], axis=1)


NEAR = 1024
FAR = 27 * 64
KEYS = NEAR + 2 * FAR


CHUNKS = [(at, min(512, KEYS - at)) for at in range(0, KEYS, 512)]


def attend_kernel(
    place_ref, idx_one_ref, idx_two_ref,
    own_ref, other_ref, up_ref, down_ref,
    inner_ref, corner_ref, outer_ref, side_ref, other_outer_ref, other_side_ref, own_two_ref,
    z_one_ref, z_two_ref, z_three_ref, up_two_ref, down_two_ref, across_ref,
    oz_one_ref, oz_two_ref, oz_three_ref, other_up_ref, other_down_ref, other_across_ref,
    out_ref, one_ref, two_ref, tall_ref, in_ref, out_strip_ref, kv_ref, kv_next_ref, s_pair_ref, s_third_ref,
):
    y = place_ref[0]
    z = place_ref[1]
    core = place_ref[2]

    tall_ref[0:128] = up_ref[256:384]
    tall_ref[1152:1280] = down_ref[256:384]
    for xs in range(4):
        tall_ref[128 + 256 * xs:384 + 256 * xs] = own_ref[xs, FINE:QUERY]
    for strip_ref, middle_ref, ends_ref, at in (
        (in_ref, inner_ref, corner_ref, 0), (out_strip_ref, outer_ref, side_ref, 512),
    ):
        strip_ref[0:64] = ends_ref[at:at + 64]
        strip_ref[64:576] = middle_ref[at:at + 512]
        strip_ref[576:640] = ends_ref[at + 64:at + 128]

    def quarter(xs, kk):
        return pl.ds(pl.multiple_of(32 * (xs & 1) + 16 * kk, 16), 16)

    def put_one(row, col, block):
        one_ref[row * 6 + col] = block

    def put_two(brow, bcol, xs, kk, block):
        two_ref[brow * 7 + bcol, quarter(xs, kk)] = block

    for m in range(2):
        kk = core if m == 0 else 1 - core
        mine = own_ref if m == 0 else other_ref
        base = ONE if m == 0 else 0
        for xs in range(4):
            put_one(2 + xs, 2 + kk, mine[xs, base:base + 64])
        for i in range(2):
            at = 128 * m + 64 * i
            put_one(i, 2 + kk, up_ref[at:at + 64])
            put_one(6 + i, 2 + kk, down_ref[at:at + 64])
    for side, middle, ends in ((core, outer_ref, side_ref), (1 - core, other_outer_ref, other_side_ref)):
        for m in range(2):
            kk = 1 - side if m == 0 else side
            for i in range(4):
                at = 256 * m + 64 * i
                put_one(2 + i, 4 * side + kk, middle[at:at + 64])
            for i in range(2):
                at = 128 * m + 64 * i
                put_one(i, 4 * side + kk, ends[at:at + 64])
                put_one(6 + i, 4 * side + kk, ends[at + 256:at + 320])
    for xs in range(4):
        for kk in range(2):
            put_two(3 + xs // 2, 3, xs, kk, own_two_ref[xs, kk])
    end = jnp.where(y >= 2, 0, 7)
    for side, twos, ups, across in (
        (core, (z_one_ref, z_two_ref, z_three_ref), (up_two_ref, down_two_ref), across_ref),
        (
            1 - core, (oz_one_ref, oz_two_ref, oz_three_ref),
            (other_up_ref, other_down_ref), other_across_ref,
        ),
    ):
        step = 2 * side - 1
        for xs in range(4):
            put_two(1 + xs // 2, 3, xs, side, ups[0][16 * xs:16 * xs + 16])
            put_two(5 + xs // 2, 3, xs, side, ups[1][16 * xs:16 * xs + 16])
        for i in range(2):
            put_two(end, 3, i, side, across[16 * i:16 * i + 16])
        for far in (1, 2, 3):
            col = 3 + far * step
            for kk in range(2):
                for xs in range(4):
                    at = 32 * xs + 16 * kk
                    put_two(3 + xs // 2, col, xs, kk, twos[far - 1][at:at + 16])
                    at = 128 * far - 64 + at
                    put_two(1 + xs // 2, col, xs, kk, ups[0][at:at + 16])
                    put_two(5 + xs // 2, col, xs, kk, ups[1][at:at + 16])
                for i in range(2):
                    at = 64 * far - 32 + 32 * i + 16 * kk
                    put_two(end, col, i, kk, across[at:at + 16])

    lane64 = iota((64, 128), 1)
    high_one, low_one = split_bias(1)
    high_two, low_two = split_bias(2)
    tok = iota((256, 128), 0)
    lane = iota((256, 128), 1)
    block = ((tok >> 7) << 1) + ((tok >> 3) & 1)
    q_feat = jnp.where((lane == block) | (lane == 4) | (lane == 5), 1.0, 0.0).astype(BF)

    def near_features(rows_wide, wide_log, col_base, tile, first_row):
        count = rows_wide << wide_log
        key = iota((count, 128), 0)
        ln = iota((count, 128), 1)
        wr = (key >> wide_log) + first_row
        wc = (key & ((1 << wide_log) - 1)) + col_base
        br, bc = ln >> 1, ln & 1
        row = 64 * y + 16 * tile - 8 + wr
        col = 32 * z + 16 * core - 8 + wc
        ok = (wr >= 8 * br) & (wr < 8 * br + 24) & (wc >= 8 * bc) & (wc < 8 * bc + 24)
        ok = ok & (row >= 0) & (row < 256) & (col >= 0) & (col < 256)
        return jnp.where(
            (ln < 4) & jnp.logical_not(ok), NEG, jnp.where(ln == 6, 1.0, 0.0)
        ).astype(BF)

    def place_rows(kv_ref, at, size, packed, features):
        kv_ref[at:at + size, 0:128] = packed[:, 0:128]
        kv_ref[at:at + size, 128:256] = features
        kv_ref[at:at + size, 256:384] = packed[:, 256:384]
        kv_ref[at:at + size, 384:512] = packed[:, 128:256]

    inner_col = 24 - 24 * core

    def gather_steps(tile, kv_ref):
        def near(source, base, stride, first, size, at, wide_log, col_base):
            def step():
                start = pl.multiple_of(base + tile * stride + first, 128)
                features = near_features(size >> wide_log, wide_log, col_base, tile, first >> wide_log)
                place_rows(kv_ref, at + first, size, source[pl.ds(start, size)], features)

            return step

        def far(j, level):
            idx_ref, win_ref, high, low = (
                (idx_one_ref, one_ref, high_one, low_one),
                (idx_two_ref, two_ref, high_two, low_two),
            )[level]

            def step():
                index = idx_ref[tile if level == 0 else tile // 2, j]
                top = jnp.where(index >= 0, jnp.float32(high), jnp.float32(NEG))
                feat = jnp.where(lane64 == 4, top, far_rest[level])
                block = win_ref[jnp.where(index >= 0, index, -1 - index)]
                place_rows(kv_ref, NEAR + level * FAR + j * 64, 64, block, feat.astype(BF))

            return step

        steps = [near(tall_ref, 0, 256, first, 128, 0, 4, 8) for first in range(0, 512, 128)]
        for first in (0, 128):
            steps.append(near(in_ref, 0, 128, first, 128, 512, 3, inner_col))
            steps.append(near(out_strip_ref, 0, 128, first, 128, 768, 3, 24 - inner_col))
        for j in range(27):
            steps += [far(j, 0), far(j, 1)]
        return steps

    low_half = lane < 64
    far_rest = [
        jnp.where(lane64 == 5, low, jnp.where(lane64 == 6, 1.0, 0.0)) for low in (low_one, low_two)
    ]

    def compute(tile, kv_ref, steps):
        steps = list(steps)
        slots = 3 * len(CHUNKS)
        share = -(-len(steps) // slots)

        def advance():
            for step in steps[:share]:
                step()
            del steps[:share]

        q_pair = jnp.concatenate([own_ref[tile, QUERY:ONE, 0:128], own_ref[tile, QUERY:ONE, 128:256]], axis=0)
        q_last = own_ref[tile, QUERY:ONE, 256:384]
        q_third = jnp.concatenate([q_last, jnp.concatenate([q_last[:, 64:], q_last[:, :64]], axis=1)], axis=0)
        zero = jnp.zeros_like(q_pair)
        lhs_pair = jnp.concatenate(
            [
                jnp.concatenate([jnp.where(low_half, q_pair, zero), q_feat], axis=1),
                jnp.concatenate([jnp.where(low_half, zero, q_pair), q_feat], axis=1),
            ],
            axis=0,
        )
        lhs_third = jnp.concatenate([q_feat, jnp.where(low_half, q_third, zero)], axis=1)

        def scores(lhs, lanes, s_ref, at, size, top):
            s = lax.dot_general(
                lhs, kv_ref[at:at + size, lanes], (((1,), (1,)), ((), ())), preferred_element_type=F32
            )
            s_ref[:, at:at + size] = s
            for c in range(0, size, 128):
                part = s[:, c:c + 128]
                top = part if top is None else jnp.maximum(top, part)
            return top

        def values(s_ref, at, size, peak, rhs, acc):
            w = jnp.exp(s_ref[:, at:at + size] - peak).astype(BF)
            part = jnp.dot(w, rhs, preferred_element_type=F32)
            return part if acc is None else acc + part

        top = None
        for at, size in CHUNKS:
            top = scores(lhs_pair, slice(0, 256), s_pair_ref, at, size, top)
            advance()
        peak = jnp.max(top, axis=1, keepdims=True)
        top = acc = None
        for at, size in CHUNKS:
            top = scores(lhs_third, slice(128, 384), s_third_ref, at, size, top)
            rhs = jnp.concatenate([kv_ref[at:at + size, 128:256], kv_ref[at:at + size, 384:512]], axis=1)
            acc = values(s_pair_ref, at, size, peak, rhs, acc)
            advance()
        out = acc[:, 128:256] / acc[:, 6:7]
        pair_out = jnp.where(low_half, out[0:256], out[256:512])
        peak = jnp.max(top, axis=1, keepdims=True)
        acc = None
        for at, size in CHUNKS:
            acc = values(s_third_ref, at, size, peak, kv_ref[at:at + size, 128:384], acc)
            advance()
        third_out = acc[:, 128:256] / acc[:, 6:7]
        out_ref[tile, :, 0:128] = pair_out[0:128].astype(BF)
        out_ref[tile, :, 128:256] = pair_out[128:256].astype(BF)
        out_ref[tile, :, 256:384] = jnp.concatenate(
            [third_out[0:128, 64:], third_out[128:256, 64:]], axis=1
        ).astype(BF)

    for step in gather_steps(0, kv_ref):
        step()

    def two_tiles(i, carry):
        compute(2 * i, kv_ref, gather_steps(2 * i + 1, kv_next_ref))
        compute(2 * i + 1, kv_next_ref, gather_steps(jnp.minimum(2 * i + 2, 3), kv_ref))
        return carry

    lax.fori_loop(0, 2, two_tiles, 0)


def call(kernel, out_shape, in_specs, scratch=(), flops=0, nbytes=0):
    return pl.pallas_call(
        kernel,
        out_shape=out_shape,
        in_specs=in_specs,
        out_specs=jax.tree.map(lambda _: VMEM, out_shape),
        scratch_shapes=scratch,
        compiler_params=pltpu.CompilerParams(vmem_limit_bytes=56 * 2**20),
        cost_estimate=pl.CostEstimate(flops=flops, bytes_accessed=nbytes, transcendentals=0),
    )


def shape(*dims):
    return jax.ShapeDtypeStruct(dims, BF)


def attend_call(*arrays):
    return call(
        attend_kernel,
        shape(4, 128, 384),
        [SMEM] * 3 + [VMEM] * 23,
        scratch=[
            pltpu.VMEM((48, 64, 384), BF),
            pltpu.VMEM((56, 64, 384), BF),
            pltpu.VMEM((1280, 384), BF),
            pltpu.VMEM((640, 384), BF),
            pltpu.VMEM((640, 384), BF),
            pltpu.VMEM((KEYS, 512), BF),
            pltpu.VMEM((KEYS, 512), BF),
            pltpu.VMEM((512, KEYS), F32),
            pltpu.VMEM((256, KEYS), F32),
        ],
        flops=12 * 256 * KEYS * 768,
        nbytes=10 << 20,
    )(*arrays)


def z_perm(step):
    pairs = []
    for z in range(8):
        if z + step < 8:
            pairs.append((2 * z + 1, 2 * (z + step)))
        if z - step >= 0:
            pairs.append((2 * z, 2 * (z - step) + 1))
    return pairs


def body(queries, keys, values, list_one, list_two):
    y = lax.axis_index("y")
    x = lax.axis_index("x")
    z = lax.axis_index("z")
    core = lax.axis_index("core")
    up = [(i, i + 1) for i in range(3)]
    down = [(i + 1, i) for i in range(3)]
    across = [(i, i ^ 2) for i in range(4)]

    entries = lax.dynamic_slice(list_one.reshape(16, 16, 27), (4 * y, 2 * z + core, 0), (4, 1, 27))[:, 0]
    where = (entries // 16 - (4 * y - 2)) * 6 + entries % 16 - (2 * z - 2)
    self_one = (2 + jnp.arange(4, dtype=jnp.int32)[:, None]) * 6 + 2 + core
    idx_one = jnp.where(entries >= 0, where, -1 - self_one)
    entries = lax.dynamic_slice(list_two.reshape(8, 8, 27), (2 * y, z, 0), (2, 1, 27))[:, 0]
    where = (entries // 8 - (2 * y - 3)) * 7 + entries % 8 - (z - 3)
    self_two = (3 + jnp.arange(2, dtype=jnp.int32)[:, None]) * 7 + 3
    idx_two = jnp.where(entries >= 0, where, -1 - self_two)
    place = jnp.stack([y, z, core]).astype(jnp.int32)

    own_two, packed = call(
        prep_kernel, [shape(4, 2, 16, 384), shape(4, PACKED, 384)], [VMEM] * 3, nbytes=4 << 20
    )(queries.reshape(256, 768), keys.reshape(256, 768), values.reshape(256, 768))

    def over_core(array):
        return lax.ppermute(array, "core", [(0, 1), (1, 0)])

    def over_z(array, step=1):
        return lax.ppermute(array, ("z", "core"), z_perm(step))

    def strips(tokens):
        rows = tokens.shape[0] // 16
        tokens = tokens.reshape(rows, 16, 384)
        left, right = tokens[:, 0:8], tokens[:, 8:16]
        inner = jnp.where(core == 0, right, left).reshape(rows * 8, 384)
        outer = jnp.where(core == 0, left, right).reshape(rows * 8, 384)
        return inner, outer

    own_two = lax.all_to_all(own_two.reshape(8, 16, 384), ("x", "core"), 0, 0, tiled=True)
    rf = lax.all_to_all(packed, "x", 0, 0, tiled=True)
    twos = own_two.reshape(128, 384)
    twos_z = [over_z(twos, step) for step in (1, 2, 3)]
    rf, idx_one, idx_two, place, *twos_z = lax.optimization_barrier(
        (rf, idx_one, idx_two, place, *twos_z)
    )

    fine = rf[:, FINE:QUERY].reshape(1024, 384)
    other = over_core(rf[:, ONE:PACKED].reshape(256, 384)).reshape(4, 64, 384)
    ones = (rf[:, ONE:PACKED], other)
    from_up = lax.ppermute(
        jnp.concatenate([t[2:4].reshape(128, 384) for t in ones] + [fine[896:1024]], axis=0), "y", up
    )
    from_down = lax.ppermute(
        jnp.concatenate([t[0:2].reshape(128, 384) for t in ones] + [fine[0:128]], axis=0), "y", down
    )
    inner_strip, outer_strip = strips(fine)
    outer = over_z(jnp.concatenate([t.reshape(256, 384) for t in ones] + [outer_strip], axis=0))
    own_two = own_two.reshape(4, 2, 16, 384)
    mine = lax.dynamic_index_in_dim(own_two, core, 1, keepdims=False).reshape(64, 384)
    near_two = jnp.concatenate([mine, *twos_z], axis=0)
    up_two = lax.ppermute(near_two, "y", up)
    down_two = lax.ppermute(near_two, "y", down)
    half = jnp.where(y < 2, 1, 0)
    halves = [lax.dynamic_index_in_dim(mine.reshape(2, 32, 384), half, 0, keepdims=False)]
    halves += [lax.dynamic_index_in_dim(t.reshape(2, 64, 384), half, 0, keepdims=False) for t in twos_z]
    across_two = lax.ppermute(jnp.concatenate(halves, axis=0), "y", across)
    inner = over_core(inner_strip)
    from_up, from_down, outer, inner, up_two, down_two, across_two = lax.optimization_barrier(
        (from_up, from_down, outer, inner, up_two, down_two, across_two)
    )

    top_inner, top_outer = strips(from_up[256:384])
    bottom_inner, bottom_outer = strips(from_down[256:384])
    side = over_z(
        jnp.concatenate([from_up[0:256], from_down[0:256], top_outer, bottom_outer], axis=0)
    )
    corner = over_core(jnp.concatenate([top_inner, bottom_inner], axis=0))
    twos_side = [*twos_z, up_two, down_two, across_two]
    others = [over_core(t) for t in twos_side]
    other_outer = over_core(outer[0:512])
    other_side = over_core(side[0:512])

    out = attend_call(
        place, idx_one, idx_two, rf, other, from_up, from_down,
        inner, corner, outer, side, other_outer, other_side, own_two, *twos_side, *others,
    )
    back = lax.all_to_all(out, "x", 0, 0, tiled=True)
    tile = call(unpack_kernel, shape(256, 768), [VMEM], nbytes=1 << 20)(back)
    return tile.reshape(16, 16, 768)


def solution(mesh):
    fine_mesh = Mesh(mesh.devices.reshape(4, 4, 8, 2), ("y", "x", "z", "core"))
    spec = P(("y", "x"), ("z", "core"), None)
    return jax.shard_map(
        body, mesh=fine_mesh, in_specs=(spec, spec, spec, P(), P()), out_specs=spec, check_vma=False
    )
```

```python
import math

import jax
import jax.numpy as jnp
import numpy as np
from jax import lax
from jax.experimental import pallas as pl
from jax.experimental.pallas import tpu as pltpu
from jax.sharding import Mesh, PartitionSpec as P

BF = jnp.bfloat16
F32 = jnp.float32
NEG = -1e30
VMEM = pl.BlockSpec(memory_space=pltpu.VMEM)
SMEM = pl.BlockSpec(memory_space=pltpu.SMEM)


def split_bias(level):
    full = 2.0 * level * math.log(2.0)
    high = float(np.float32(full).astype(BF))
    return high, float(np.float32(full - high).astype(BF))


def iota(shape, dim):
    return lax.broadcasted_iota(jnp.int32, shape, dim)


FINE, QUERY, ONE, TWO, PACKED = 0, 256, 384, 448, 464


def prep_kernel(q_ref, k_ref, v_ref, out_ref):
    row = iota((80, 256), 0)
    tok = iota((80, 256), 1)
    trow, tcol = tok >> 4, tok & 15
    one = (row < 64) & ((trow >> 1) == (row >> 3)) & ((tcol >> 1) == (row & 7))
    rest = row - 64
    two = (row >= 64) & ((trow >> 2) == (rest >> 2)) & ((tcol >> 2) == (rest & 3))
    pool = jnp.where(one, 0.25, jnp.where(two, 0.0625, 0.0)).astype(BF)
    k = k_ref[...]
    v = v_ref[...]
    kc = jnp.dot(pool, k, preferred_element_type=F32).astype(BF)
    vc = jnp.dot(pool, v, preferred_element_type=F32).astype(BF)
    q = (q_ref[...].astype(F32) * 0.125).astype(BF)
    for j in range(4):
        pair = slice(128 * j, 128 * j + 128)
        third = slice(512 + 64 * j, 576 + 64 * j)
        out_ref[j, FINE:QUERY, 0:128] = k[:, pair]
        out_ref[j, FINE:QUERY, 128:256] = v[:, pair]
        out_ref[j, FINE:QUERY, 256:384] = jnp.concatenate([k[:, third], v[:, third]], axis=1)
        out_ref[j, QUERY:ONE, 0:128] = q[0:128, pair]
        out_ref[j, QUERY:ONE, 128:256] = q[128:256, pair]
        out_ref[j, QUERY:ONE, 256:384] = jnp.concatenate(
            [q[0:128, third], q[128:256, third]], axis=1
        )
        out_ref[j, ONE:PACKED, 0:128] = kc[:, pair]
        out_ref[j, ONE:PACKED, 128:256] = vc[:, pair]
        out_ref[j, ONE:PACKED, 256:384] = jnp.concatenate([kc[:, third], vc[:, third]], axis=1)


def unpack_kernel(o_ref, out_ref):
    for j in range(4):
        pair = slice(128 * j, 128 * j + 128)
        out_ref[0:128, pair] = o_ref[j, :, 0:128]
        out_ref[128:256, pair] = o_ref[j, :, 128:256]
    lane = iota((128, 128), 1)
    for j in (0, 2):
        first = o_ref[j, :, 256:384]
        second = o_ref[j + 1, :, 256:384]
        lanes = slice(512 + 64 * j, 640 + 64 * j)
        out_ref[0:128, lanes] = jnp.concatenate([first[:, :64], second[:, :64]], axis=1)
        out_ref[128:256, lanes] = jnp.concatenate([first[:, 64:], second[:, 64:]], axis=1)


NEAR = 1024
FAR = 27 * 64
KEYS = NEAR + 2 * FAR


CHUNKS = [(at, min(512, KEYS - at)) for at in range(0, KEYS, 512)]


def attend_kernel(
    place_ref, idx_one_ref, idx_two_ref,
    own_ref, other_ref, up_ref, down_ref, inner_ref, side_ref, other_side_ref,
    row_ref, up_two_ref, down_two_ref, across_ref,
    other_row_ref, other_up_ref, other_down_ref, other_across_ref,
    out_ref, one_ref, two_ref, tall_ref, kv_ref, kv_next_ref, s_pair_ref, s_third_ref,
):
    y = place_ref[0]
    z = place_ref[1]
    core = place_ref[2]

    tall_ref[0:128] = up_ref[256:384]
    tall_ref[1152:1280] = down_ref[256:384]
    for xs in range(4):
        tall_ref[128 + 256 * xs:384 + 256 * xs] = own_ref[xs, FINE:QUERY]

    def quarter(xs, kk):
        return pl.ds(pl.multiple_of(32 * (xs & 1) + 16 * kk, 16), 16)

    def put_one(row, col, block):
        one_ref[row * 6 + col] = block

    for m in range(2):
        kk = core if m == 0 else 1 - core
        mine = own_ref if m == 0 else other_ref
        base = ONE if m == 0 else 0
        for xs in range(4):
            put_one(2 + xs, 2 + kk, mine[xs, base:base + 64])
        for i in range(2):
            at = 128 * m + 64 * i
            put_one(i, 2 + kk, up_ref[at:at + 64])
            put_one(6 + i, 2 + kk, down_ref[at:at + 64])
    for side, one_side in ((core, side_ref), (1 - core, other_side_ref)):
        for m in range(2):
            kk = 1 - side if m == 0 else side
            for i in range(4):
                at = 256 * m + 64 * i
                put_one(2 + i, 4 * side + kk, one_side[at:at + 64])
            for i in range(2):
                at = 512 + 128 * m + 64 * i
                put_one(i, 4 * side + kk, one_side[at:at + 64])
                put_one(6 + i, 4 * side + kk, one_side[at + 256:at + 320])
    end = jnp.where(y >= 2, 2 * y - 1, 2 * y + 6)
    for kk, row, ups, downs, across in (
        (core, row_ref, up_two_ref, down_two_ref, across_ref),
        (1 - core, other_row_ref, other_up_ref, other_down_ref, other_across_ref),
    ):
        for col in range(8):
            for xs in range(4):
                at = 64 * col + 16 * xs
                brow = 2 * y + 2 + xs // 2
                two_ref[brow * 8 + col, quarter(xs, kk)] = row[at:at + 16]
                two_ref[(brow - 2) * 8 + col, quarter(xs, kk)] = ups[at:at + 16]
                two_ref[(brow + 2) * 8 + col, quarter(xs, kk)] = downs[at:at + 16]
            for i in range(2):
                at = 32 * col + 16 * i
                two_ref[end * 8 + col, quarter(i, kk)] = across[at:at + 16]

    lane64 = iota((64, 128), 1)
    high_one, low_one = split_bias(1)
    high_two, low_two = split_bias(2)
    tok = iota((256, 128), 0)
    lane = iota((256, 128), 1)
    block = ((tok >> 7) << 1) + ((tok >> 3) & 1)
    q_feat = jnp.where((lane == block) | (lane == 4) | (lane == 5), 1.0, 0.0).astype(BF)

    def near_features(rows_wide, wide_log, col_base, tile, first_row):
        count = rows_wide << wide_log
        key = iota((count, 128), 0)
        ln = iota((count, 128), 1)
        wr = (key >> wide_log) + first_row
        wc = (key & ((1 << wide_log) - 1)) + col_base
        br, bc = ln >> 1, ln & 1
        row = 64 * y + 16 * tile - 8 + wr
        col = 32 * z + 16 * core - 8 + wc
        ok = (wr >= 8 * br) & (wr < 8 * br + 24) & (wc >= 8 * bc) & (wc < 8 * bc + 24)
        ok = ok & (row >= 0) & (row < 256) & (col >= 0) & (col < 256)
        return jnp.where(
            (ln < 4) & jnp.logical_not(ok), NEG, jnp.where(ln == 6, 1.0, 0.0)
        ).astype(BF)

    def place_rows(kv_ref, at, size, packed, features):
        kv_ref[at:at + size, 0:128] = packed[:, 0:128]
        kv_ref[at:at + size, 128:256] = features
        kv_ref[at:at + size, 256:384] = packed[:, 256:384]
        kv_ref[at:at + size, 384:512] = packed[:, 128:256]

    inner_col = 24 - 24 * core

    def gather_steps(tile, kv_ref):
        def near(source, base, stride, first, size, at, wide_log, col_base):
            def step():
                start = pl.multiple_of(base + tile * stride + first, 128)
                features = near_features(size >> wide_log, wide_log, col_base, tile, first >> wide_log)
                place_rows(kv_ref, at + first, size, source[pl.ds(start, size)], features)

            return step

        def far(j, level):
            idx_ref, win_ref, high, low = (
                (idx_one_ref, one_ref, high_one, low_one),
                (idx_two_ref, two_ref, high_two, low_two),
            )[level]

            def step():
                index = idx_ref[tile if level == 0 else tile // 2, j]
                top = jnp.where(index >= 0, jnp.float32(high), jnp.float32(NEG))
                feat = jnp.where(lane64 == 4, top, far_rest[level])
                block = win_ref[jnp.where(index >= 0, index, -1 - index)]
                place_rows(kv_ref, NEAR + level * FAR + j * 64, 64, block, feat.astype(BF))

            return step

        steps = [near(tall_ref, 0, 256, first, 128, 0, 4, 8) for first in range(0, 512, 128)]
        for first in (0, 128):
            steps.append(near(inner_ref, 0, 128, first, 128, 512, 3, inner_col))
            steps.append(near(side_ref, 1024, 128, first, 128, 768, 3, 24 - inner_col))
        for j in range(27):
            steps += [far(j, 0), far(j, 1)]
        return steps

    low_half = lane < 64
    far_rest = [
        jnp.where(lane64 == 5, low, jnp.where(lane64 == 6, 1.0, 0.0)) for low in (low_one, low_two)
    ]

    def compute(tile, kv_ref, steps):
        steps = list(steps)
        slots = 3 * len(CHUNKS)
        share = -(-len(steps) // slots)

        def advance():
            for step in steps[:share]:
                step()
            del steps[:share]

        q_pair = jnp.concatenate([own_ref[tile, QUERY:ONE, 0:128], own_ref[tile, QUERY:ONE, 128:256]], axis=0)
        q_last = own_ref[tile, QUERY:ONE, 256:384]
        q_third = jnp.concatenate([q_last, jnp.concatenate([q_last[:, 64:], q_last[:, :64]], axis=1)], axis=0)
        zero = jnp.zeros_like(q_pair)
        lhs_pair = jnp.concatenate(
            [
                jnp.concatenate([jnp.where(low_half, q_pair, zero), q_feat], axis=1),
                jnp.concatenate([jnp.where(low_half, zero, q_pair), q_feat], axis=1),
            ],
            axis=0,
        )
        lhs_third = jnp.concatenate([q_feat, jnp.where(low_half, q_third, zero)], axis=1)

        def scores(lhs, lanes, s_ref, at, size, top):
            s = lax.dot_general(
                lhs, kv_ref[at:at + size, lanes], (((1,), (1,)), ((), ())), preferred_element_type=F32
            )
            s_ref[:, at:at + size] = s
            for c in range(0, size, 128):
                part = s[:, c:c + 128]
                top = part if top is None else jnp.maximum(top, part)
            return top

        def values(s_ref, at, size, peak, rhs, acc):
            w = jnp.exp(s_ref[:, at:at + size] - peak).astype(BF)
            part = jnp.dot(w, rhs, preferred_element_type=F32)
            return part if acc is None else acc + part

        top = None
        for at, size in CHUNKS:
            top = scores(lhs_pair, slice(0, 256), s_pair_ref, at, size, top)
            advance()
        peak = jnp.max(top, axis=1, keepdims=True)
        top = acc = None
        for at, size in CHUNKS:
            top = scores(lhs_third, slice(128, 384), s_third_ref, at, size, top)
            rhs = jnp.concatenate([kv_ref[at:at + size, 128:256], kv_ref[at:at + size, 384:512]], axis=1)
            acc = values(s_pair_ref, at, size, peak, rhs, acc)
            advance()
        out = acc[:, 128:256] / acc[:, 6:7]
        pair_out = jnp.where(low_half, out[0:256], out[256:512])
        peak = jnp.max(top, axis=1, keepdims=True)
        acc = None
        for at, size in CHUNKS:
            acc = values(s_third_ref, at, size, peak, kv_ref[at:at + size, 128:384], acc)
            advance()
        third_out = acc[:, 128:256] / acc[:, 6:7]
        out_ref[tile, :, 0:128] = pair_out[0:128].astype(BF)
        out_ref[tile, :, 128:256] = pair_out[128:256].astype(BF)
        out_ref[tile, :, 256:384] = jnp.concatenate(
            [third_out[0:128, 64:], third_out[128:256, 64:]], axis=1
        ).astype(BF)

    for step in gather_steps(0, kv_ref):
        step()

    def two_tiles(i, carry):
        compute(2 * i, kv_ref, gather_steps(2 * i + 1, kv_next_ref))
        compute(2 * i + 1, kv_next_ref, gather_steps(jnp.minimum(2 * i + 2, 3), kv_ref))
        return carry

    lax.fori_loop(0, 2, two_tiles, 0)


def call(kernel, out_shape, in_specs, scratch=(), flops=0, nbytes=0):
    return pl.pallas_call(
        kernel,
        out_shape=out_shape,
        in_specs=in_specs,
        out_specs=jax.tree.map(lambda _: VMEM, out_shape),
        scratch_shapes=scratch,
        compiler_params=pltpu.CompilerParams(vmem_limit_bytes=56 * 2**20),
        cost_estimate=pl.CostEstimate(flops=flops, bytes_accessed=nbytes, transcendentals=0),
    )


def shape(*dims):
    return jax.ShapeDtypeStruct(dims, BF)


def attend_call(*arrays):
    return call(
        attend_kernel,
        shape(4, 128, 384),
        [SMEM] * 3 + [VMEM] * 15,
        scratch=[
            pltpu.VMEM((48, 64, 384), BF),
            pltpu.VMEM((96, 64, 384), BF),
            pltpu.VMEM((1280, 384), BF),
            pltpu.VMEM((KEYS, 512), BF),
            pltpu.VMEM((KEYS, 512), BF),
            pltpu.VMEM((512, KEYS), F32),
            pltpu.VMEM((256, KEYS), F32),
        ],
        flops=12 * 256 * KEYS * 768,
        nbytes=10 << 20,
    )(*arrays)


def z_perm(step):
    pairs = []
    for z in range(8):
        if z + step < 8:
            pairs.append((2 * z + 1, 2 * (z + step)))
        if z - step >= 0:
            pairs.append((2 * z, 2 * (z - step) + 1))
    return pairs


def body(queries, keys, values, list_one, list_two):
    y = lax.axis_index("y")
    x = lax.axis_index("x")
    z = lax.axis_index("z")
    core = lax.axis_index("core")
    up = [(i, i + 1) for i in range(3)]
    down = [(i + 1, i) for i in range(3)]
    across = [(i, i ^ 2) for i in range(4)]

    entries = lax.dynamic_slice(list_one.reshape(16, 16, 27), (4 * y, 2 * z + core, 0), (4, 1, 27))[:, 0]
    where = (entries // 16 - (4 * y - 2)) * 6 + entries % 16 - (2 * z - 2)
    self_one = (2 + jnp.arange(4, dtype=jnp.int32)[:, None]) * 6 + 2 + core
    idx_one = jnp.where(entries >= 0, where, -1 - self_one)
    entries = lax.dynamic_slice(list_two.reshape(8, 8, 27), (2 * y, z, 0), (2, 1, 27))[:, 0]
    self_two = (2 * y + 2 + jnp.arange(2, dtype=jnp.int32)[:, None]) * 8 + z
    idx_two = jnp.where(entries >= 0, entries + 16, -1 - self_two)
    place = jnp.stack([y, z, core]).astype(jnp.int32)

    packed = call(prep_kernel, shape(4, PACKED, 384), [VMEM] * 3, nbytes=4 << 20)(
        queries.reshape(256, 768), keys.reshape(256, 768), values.reshape(256, 768)
    )
    rf = lax.all_to_all(packed, "x", 0, 0, tiled=True)
    rf, idx_one, idx_two, place = lax.optimization_barrier((rf, idx_one, idx_two, place))

    def over_core(array):
        return lax.ppermute(array, "core", [(0, 1), (1, 0)])

    def over_z(array, step=1):
        return lax.ppermute(array, ("z", "core"), z_perm(step))

    def strips(tokens):
        rows = tokens.shape[0] // 16
        tokens = tokens.reshape(rows, 16, 384)
        left, right = tokens[:, 0:8], tokens[:, 8:16]
        inner = jnp.where(core == 0, right, left).reshape(rows * 8, 384)
        outer = jnp.where(core == 0, left, right).reshape(rows * 8, 384)
        return inner, outer

    fine = rf[:, FINE:QUERY].reshape(1024, 384)
    other = over_core(rf[:, ONE:TWO].reshape(256, 384)).reshape(4, 64, 384)
    ones = (rf[:, ONE:TWO], other)
    two = rf[:, TWO:PACKED].reshape(1, 64, 384)
    row_two = lax.all_to_all(jnp.broadcast_to(two, (8, 64, 384)), "z", 0, 0, tiled=True)
    from_up = lax.ppermute(
        jnp.concatenate([t[2:4].reshape(128, 384) for t in ones] + [fine[896:1024]], axis=0), "y", up
    )
    from_down = lax.ppermute(
        jnp.concatenate([t[0:2].reshape(128, 384) for t in ones] + [fine[0:128]], axis=0), "y", down
    )
    row_two, from_up, from_down = lax.optimization_barrier((row_two, from_up, from_down))

    top_inner, top_outer = strips(from_up[256:384])
    middle_inner, middle_outer = strips(fine)
    bottom_inner, bottom_outer = strips(from_down[256:384])
    side = over_z(
        jnp.concatenate(
            [t.reshape(256, 384) for t in ones]
            + [from_up[0:256], from_down[0:256], top_outer, middle_outer, bottom_outer],
            axis=0,
        )
    )
    inner = over_core(jnp.concatenate([top_inner, middle_inner, bottom_inner], axis=0))
    up_two = lax.ppermute(row_two.reshape(512, 384), "y", up)
    down_two = lax.ppermute(row_two.reshape(512, 384), "y", down)
    half = jnp.where(y < 2, 1, 0)
    across_two = lax.ppermute(
        lax.dynamic_index_in_dim(row_two.reshape(8, 2, 32, 384), half, 1, keepdims=False).reshape(256, 384),
        "y",
        across,
    )
    other_row = over_core(row_two.reshape(512, 384))
    side, up_two, down_two, across_two, inner, other_row = lax.optimization_barrier(
        (side, up_two, down_two, across_two, inner, other_row)
    )

    other_side = over_core(side[0:1024])
    others = [over_core(t) for t in (up_two, down_two, across_two)]

    out = attend_call(
        place, idx_one, idx_two, rf, other, from_up, from_down, inner, side, other_side,
        row_two.reshape(512, 384), up_two, down_two, across_two, other_row, *others,
    )
    back = lax.all_to_all(out, "x", 0, 0, tiled=True)
    tile = call(unpack_kernel, shape(256, 768), [VMEM], nbytes=1 << 20)(back)
    return tile.reshape(16, 16, 768)


def solution(mesh):
    fine_mesh = Mesh(mesh.devices.reshape(4, 4, 8, 2), ("y", "x", "z", "core"))
    spec = P(("y", "x"), ("z", "core"), None)
    return jax.shard_map(
        body, mesh=fine_mesh, in_specs=(spec, spec, spec, P(), P()), out_specs=spec, check_vma=False
    )
```

```python
import math

import jax
import jax.numpy as jnp
import numpy as np
from jax import lax
from jax.experimental import pallas as pl
from jax.experimental.pallas import tpu as pltpu
from jax.sharding import Mesh, PartitionSpec as P

BF = jnp.bfloat16
F32 = jnp.float32
NEG = -1e30
VMEM = pl.BlockSpec(memory_space=pltpu.VMEM)
SMEM = pl.BlockSpec(memory_space=pltpu.SMEM)


def split_bias(level):
    full = 2.0 * level * math.log(2.0)
    high = float(np.float32(full).astype(BF))
    return high, float(np.float32(full - high).astype(BF))


def iota(shape, dim):
    return lax.broadcasted_iota(jnp.int32, shape, dim)


FINE, QUERY, ONE, TWO, PACKED = 0, 256, 384, 448, 464


def prep_kernel(q_ref, k_ref, v_ref, out_ref):
    row = iota((80, 256), 0)
    tok = iota((80, 256), 1)
    trow, tcol = tok >> 4, tok & 15
    one = (row < 64) & ((trow >> 1) == (row >> 3)) & ((tcol >> 1) == (row & 7))
    rest = row - 64
    two = (row >= 64) & ((trow >> 2) == (rest >> 2)) & ((tcol >> 2) == (rest & 3))
    pool = jnp.where(one, 0.25, jnp.where(two, 0.0625, 0.0)).astype(BF)
    k = k_ref[...]
    v = v_ref[...]
    kc = jnp.dot(pool, k, preferred_element_type=F32).astype(BF)
    vc = jnp.dot(pool, v, preferred_element_type=F32).astype(BF)
    q = (q_ref[...].astype(F32) * 0.125).astype(BF)
    for j in range(4):
        pair = slice(128 * j, 128 * j + 128)
        third = slice(512 + 64 * j, 576 + 64 * j)
        out_ref[j, FINE:QUERY, 0:128] = k[:, pair]
        out_ref[j, FINE:QUERY, 128:256] = v[:, pair]
        out_ref[j, FINE:QUERY, 256:384] = jnp.concatenate([k[:, third], v[:, third]], axis=1)
        out_ref[j, QUERY:ONE, 0:128] = q[0:128, pair]
        out_ref[j, QUERY:ONE, 128:256] = q[128:256, pair]
        out_ref[j, QUERY:ONE, 256:384] = jnp.concatenate(
            [q[0:128, third], q[128:256, third]], axis=1
        )
        out_ref[j, ONE:PACKED, 0:128] = kc[:, pair]
        out_ref[j, ONE:PACKED, 128:256] = vc[:, pair]
        out_ref[j, ONE:PACKED, 256:384] = jnp.concatenate([kc[:, third], vc[:, third]], axis=1)


def unpack_kernel(o_ref, out_ref):
    for j in range(4):
        pair = slice(128 * j, 128 * j + 128)
        out_ref[0:128, pair] = o_ref[j, :, 0:128]
        out_ref[128:256, pair] = o_ref[j, :, 128:256]
    lane = iota((128, 128), 1)
    for j in (0, 2):
        first = o_ref[j, :, 256:384]
        second = o_ref[j + 1, :, 256:384]
        lanes = slice(512 + 64 * j, 640 + 64 * j)
        out_ref[0:128, lanes] = jnp.concatenate([first[:, :64], second[:, :64]], axis=1)
        out_ref[128:256, lanes] = jnp.concatenate([first[:, 64:], second[:, 64:]], axis=1)


NEAR = 1024
FAR = 27 * 64
KEYS = NEAR + 2 * FAR


CHUNKS = [(at, min(512, KEYS - at)) for at in range(0, KEYS, 512)]


def attend_kernel(
    place_ref, idx_one_ref, idx_two_ref,
    own_ref, other_ref, up_ref, down_ref,
    inner_ref, outer_ref, side_ref, other_outer_ref, other_side_ref,
    row_ref, up_two_ref, down_two_ref, across_ref,
    other_row_ref, other_up_ref, other_down_ref, other_across_ref,
    out_ref, one_ref, two_ref, tall_ref, strip_ref, kv_ref, kv_next_ref, s_pair_ref, s_third_ref,
):
    y = place_ref[0]
    z = place_ref[1]
    core = place_ref[2]

    tall_ref[0:128] = up_ref[256:384]
    tall_ref[1152:1280] = down_ref[256:384]
    for xs in range(4):
        tall_ref[128 + 256 * xs:384 + 256 * xs] = own_ref[xs, FINE:QUERY]

    strip_ref[0:64] = side_ref[512:576]
    strip_ref[64:576] = outer_ref[512:1024]
    strip_ref[576:640] = side_ref[576:640]

    def quarter(xs, kk):
        return pl.ds(pl.multiple_of(32 * (xs & 1) + 16 * kk, 16), 16)

    def put_one(row, col, block):
        one_ref[row * 6 + col] = block

    for m in range(2):
        kk = core if m == 0 else 1 - core
        mine = own_ref if m == 0 else other_ref
        base = ONE if m == 0 else 0
        for xs in range(4):
            put_one(2 + xs, 2 + kk, mine[xs, base:base + 64])
        for i in range(2):
            at = 128 * m + 64 * i
            put_one(i, 2 + kk, up_ref[at:at + 64])
            put_one(6 + i, 2 + kk, down_ref[at:at + 64])
    for side, middle, ends in ((core, outer_ref, side_ref), (1 - core, other_outer_ref, other_side_ref)):
        for m in range(2):
            kk = 1 - side if m == 0 else side
            for i in range(4):
                at = 256 * m + 64 * i
                put_one(2 + i, 4 * side + kk, middle[at:at + 64])
            for i in range(2):
                at = 128 * m + 64 * i
                put_one(i, 4 * side + kk, ends[at:at + 64])
                put_one(6 + i, 4 * side + kk, ends[at + 256:at + 320])
    end = jnp.where(y >= 2, 2 * y - 1, 2 * y + 6)
    for kk, row, ups, downs, across in (
        (core, row_ref, up_two_ref, down_two_ref, across_ref),
        (1 - core, other_row_ref, other_up_ref, other_down_ref, other_across_ref),
    ):
        for col in range(8):
            for xs in range(4):
                at = 64 * col + 16 * xs
                brow = 2 * y + 2 + xs // 2
                two_ref[brow * 8 + col, quarter(xs, kk)] = row[at:at + 16]
                two_ref[(brow - 2) * 8 + col, quarter(xs, kk)] = ups[at:at + 16]
                two_ref[(brow + 2) * 8 + col, quarter(xs, kk)] = downs[at:at + 16]
            for i in range(2):
                at = 32 * col + 16 * i
                two_ref[end * 8 + col, quarter(i, kk)] = across[at:at + 16]

    lane64 = iota((64, 128), 1)
    high_one, low_one = split_bias(1)
    high_two, low_two = split_bias(2)
    tok = iota((256, 128), 0)
    lane = iota((256, 128), 1)
    block = ((tok >> 7) << 1) + ((tok >> 3) & 1)
    q_feat = jnp.where((lane == block) | (lane == 4) | (lane == 5), 1.0, 0.0).astype(BF)

    def near_features(rows_wide, wide_log, col_base, tile, first_row):
        count = rows_wide << wide_log
        key = iota((count, 128), 0)
        ln = iota((count, 128), 1)
        wr = (key >> wide_log) + first_row
        wc = (key & ((1 << wide_log) - 1)) + col_base
        br, bc = ln >> 1, ln & 1
        row = 64 * y + 16 * tile - 8 + wr
        col = 32 * z + 16 * core - 8 + wc
        ok = (wr >= 8 * br) & (wr < 8 * br + 24) & (wc >= 8 * bc) & (wc < 8 * bc + 24)
        ok = ok & (row >= 0) & (row < 256) & (col >= 0) & (col < 256)
        return jnp.where(
            (ln < 4) & jnp.logical_not(ok), NEG, jnp.where(ln == 6, 1.0, 0.0)
        ).astype(BF)

    def place_rows(kv_ref, at, size, packed, features):
        kv_ref[at:at + size, 0:128] = packed[:, 0:128]
        kv_ref[at:at + size, 128:256] = features
        kv_ref[at:at + size, 256:384] = packed[:, 256:384]
        kv_ref[at:at + size, 384:512] = packed[:, 128:256]

    inner_col = 24 - 24 * core

    def gather_steps(tile, kv_ref):
        def near(source, base, stride, first, size, at, wide_log, col_base):
            def step():
                start = pl.multiple_of(base + tile * stride + first, 128)
                features = near_features(size >> wide_log, wide_log, col_base, tile, first >> wide_log)
                place_rows(kv_ref, at + first, size, source[pl.ds(start, size)], features)

            return step

        def far(j, level):
            idx_ref, win_ref, high, low = (
                (idx_one_ref, one_ref, high_one, low_one),
                (idx_two_ref, two_ref, high_two, low_two),
            )[level]

            def step():
                index = idx_ref[tile if level == 0 else tile // 2, j]
                top = jnp.where(index >= 0, jnp.float32(high), jnp.float32(NEG))
                feat = jnp.where(lane64 == 4, top, far_rest[level])
                block = win_ref[jnp.where(index >= 0, index, -1 - index)]
                place_rows(kv_ref, NEAR + level * FAR + j * 64, 64, block, feat.astype(BF))

            return step

        steps = [near(tall_ref, 0, 256, first, 128, 0, 4, 8) for first in range(0, 512, 128)]
        for first in (0, 128):
            steps.append(near(inner_ref, 0, 128, first, 128, 512, 3, inner_col))
            steps.append(near(strip_ref, 0, 128, first, 128, 768, 3, 24 - inner_col))
        for j in range(27):
            steps += [far(j, 0), far(j, 1)]
        return steps

    low_half = lane < 64
    far_rest = [
        jnp.where(lane64 == 5, low, jnp.where(lane64 == 6, 1.0, 0.0)) for low in (low_one, low_two)
    ]

    def compute(tile, kv_ref, steps):
        steps = list(steps)
        slots = 3 * len(CHUNKS)
        share = -(-len(steps) // slots)

        def advance():
            for step in steps[:share]:
                step()
            del steps[:share]

        q_pair = jnp.concatenate([own_ref[tile, QUERY:ONE, 0:128], own_ref[tile, QUERY:ONE, 128:256]], axis=0)
        q_last = own_ref[tile, QUERY:ONE, 256:384]
        q_third = jnp.concatenate([q_last, jnp.concatenate([q_last[:, 64:], q_last[:, :64]], axis=1)], axis=0)
        zero = jnp.zeros_like(q_pair)
        lhs_pair = jnp.concatenate(
            [
                jnp.concatenate([jnp.where(low_half, q_pair, zero), q_feat], axis=1),
                jnp.concatenate([jnp.where(low_half, zero, q_pair), q_feat], axis=1),
            ],
            axis=0,
        )
        lhs_third = jnp.concatenate([q_feat, jnp.where(low_half, q_third, zero)], axis=1)

        def scores(lhs, lanes, s_ref, at, size, top):
            s = lax.dot_general(
                lhs, kv_ref[at:at + size, lanes], (((1,), (1,)), ((), ())), preferred_element_type=F32
            )
            s_ref[:, at:at + size] = s
            for c in range(0, size, 128):
                part = s[:, c:c + 128]
                top = part if top is None else jnp.maximum(top, part)
            return top

        def values(s_ref, at, size, peak, rhs, acc):
            w = jnp.exp(s_ref[:, at:at + size] - peak).astype(BF)
            part = jnp.dot(w, rhs, preferred_element_type=F32)
            return part if acc is None else acc + part

        top = None
        for at, size in CHUNKS:
            top = scores(lhs_pair, slice(0, 256), s_pair_ref, at, size, top)
            advance()
        peak = jnp.max(top, axis=1, keepdims=True)
        top = acc = None
        for at, size in CHUNKS:
            top = scores(lhs_third, slice(128, 384), s_third_ref, at, size, top)
            rhs = jnp.concatenate([kv_ref[at:at + size, 128:256], kv_ref[at:at + size, 384:512]], axis=1)
            acc = values(s_pair_ref, at, size, peak, rhs, acc)
            advance()
        out = acc[:, 128:256] / acc[:, 6:7]
        pair_out = jnp.where(low_half, out[0:256], out[256:512])
        peak = jnp.max(top, axis=1, keepdims=True)
        acc = None
        for at, size in CHUNKS:
            acc = values(s_third_ref, at, size, peak, kv_ref[at:at + size, 128:384], acc)
            advance()
        third_out = acc[:, 128:256] / acc[:, 6:7]
        out_ref[tile, :, 0:128] = pair_out[0:128].astype(BF)
        out_ref[tile, :, 128:256] = pair_out[128:256].astype(BF)
        out_ref[tile, :, 256:384] = jnp.concatenate(
            [third_out[0:128, 64:], third_out[128:256, 64:]], axis=1
        ).astype(BF)

    for step in gather_steps(0, kv_ref):
        step()

    def two_tiles(i, carry):
        compute(2 * i, kv_ref, gather_steps(2 * i + 1, kv_next_ref))
        compute(2 * i + 1, kv_next_ref, gather_steps(jnp.minimum(2 * i + 2, 3), kv_ref))
        return carry

    lax.fori_loop(0, 2, two_tiles, 0)


def call(kernel, out_shape, in_specs, scratch=(), flops=0, nbytes=0):
    return pl.pallas_call(
        kernel,
        out_shape=out_shape,
        in_specs=in_specs,
        out_specs=jax.tree.map(lambda _: VMEM, out_shape),
        scratch_shapes=scratch,
        compiler_params=pltpu.CompilerParams(vmem_limit_bytes=56 * 2**20),
        cost_estimate=pl.CostEstimate(flops=flops, bytes_accessed=nbytes, transcendentals=0),
    )


def shape(*dims):
    return jax.ShapeDtypeStruct(dims, BF)


def attend_call(*arrays):
    return call(
        attend_kernel,
        shape(4, 128, 384),
        [SMEM] * 3 + [VMEM] * 17,
        scratch=[
            pltpu.VMEM((48, 64, 384), BF),
            pltpu.VMEM((96, 64, 384), BF),
            pltpu.VMEM((1280, 384), BF),
            pltpu.VMEM((640, 384), BF),
            pltpu.VMEM((KEYS, 512), BF),
            pltpu.VMEM((KEYS, 512), BF),
            pltpu.VMEM((512, KEYS), F32),
            pltpu.VMEM((256, KEYS), F32),
        ],
        flops=12 * 256 * KEYS * 768,
        nbytes=10 << 20,
    )(*arrays)


def z_perm(step):
    pairs = []
    for z in range(8):
        if z + step < 8:
            pairs.append((2 * z + 1, 2 * (z + step)))
        if z - step >= 0:
            pairs.append((2 * z, 2 * (z - step) + 1))
    return pairs


def body(queries, keys, values, list_one, list_two):
    y = lax.axis_index("y")
    x = lax.axis_index("x")
    z = lax.axis_index("z")
    core = lax.axis_index("core")
    up = [(i, i + 1) for i in range(3)]
    down = [(i + 1, i) for i in range(3)]
    across = [(i, i ^ 2) for i in range(4)]

    entries = lax.dynamic_slice(list_one.reshape(16, 16, 27), (4 * y, 2 * z + core, 0), (4, 1, 27))[:, 0]
    where = (entries // 16 - (4 * y - 2)) * 6 + entries % 16 - (2 * z - 2)
    self_one = (2 + jnp.arange(4, dtype=jnp.int32)[:, None]) * 6 + 2 + core
    idx_one = jnp.where(entries >= 0, where, -1 - self_one)
    entries = lax.dynamic_slice(list_two.reshape(8, 8, 27), (2 * y, z, 0), (2, 1, 27))[:, 0]
    self_two = (2 * y + 2 + jnp.arange(2, dtype=jnp.int32)[:, None]) * 8 + z
    idx_two = jnp.where(entries >= 0, entries + 16, -1 - self_two)
    place = jnp.stack([y, z, core]).astype(jnp.int32)

    packed = call(prep_kernel, shape(4, PACKED, 384), [VMEM] * 3, nbytes=4 << 20)(
        queries.reshape(256, 768), keys.reshape(256, 768), values.reshape(256, 768)
    )
    rf = lax.all_to_all(packed, "x", 0, 0, tiled=True)
    rf, idx_one, idx_two, place = lax.optimization_barrier((rf, idx_one, idx_two, place))

    def over_core(array):
        return lax.ppermute(array, "core", [(0, 1), (1, 0)])

    def over_z(array, step=1):
        return lax.ppermute(array, ("z", "core"), z_perm(step))

    def strips(tokens):
        rows = tokens.shape[0] // 16
        tokens = tokens.reshape(rows, 16, 384)
        left, right = tokens[:, 0:8], tokens[:, 8:16]
        inner = jnp.where(core == 0, right, left).reshape(rows * 8, 384)
        outer = jnp.where(core == 0, left, right).reshape(rows * 8, 384)
        return inner, outer

    fine = rf[:, FINE:QUERY].reshape(1024, 384)
    other = over_core(rf[:, ONE:TWO].reshape(256, 384)).reshape(4, 64, 384)
    ones = (rf[:, ONE:TWO], other)
    two = rf[:, TWO:PACKED].reshape(1, 64, 384)
    row_two = lax.all_to_all(jnp.broadcast_to(two, (8, 64, 384)), "z", 0, 0, tiled=True)
    from_up = lax.ppermute(
        jnp.concatenate([t[2:4].reshape(128, 384) for t in ones] + [fine[896:1024]], axis=0), "y", up
    )
    from_down = lax.ppermute(
        jnp.concatenate([t[0:2].reshape(128, 384) for t in ones] + [fine[0:128]], axis=0), "y", down
    )
    middle_inner, middle_outer = strips(fine)
    outer = over_z(jnp.concatenate([t.reshape(256, 384) for t in ones] + [middle_outer], axis=0))
    row_two, from_up, from_down, outer = lax.optimization_barrier((row_two, from_up, from_down, outer))

    top_inner, top_outer = strips(from_up[256:384])
    bottom_inner, bottom_outer = strips(from_down[256:384])
    side = over_z(
        jnp.concatenate([from_up[0:256], from_down[0:256], top_outer, bottom_outer], axis=0)
    )
    inner = over_core(jnp.concatenate([top_inner, middle_inner, bottom_inner], axis=0))
    up_two = lax.ppermute(row_two.reshape(512, 384), "y", up)
    down_two = lax.ppermute(row_two.reshape(512, 384), "y", down)
    half = jnp.where(y < 2, 1, 0)
    across_two = lax.ppermute(
        lax.dynamic_index_in_dim(row_two.reshape(8, 2, 32, 384), half, 1, keepdims=False).reshape(256, 384),
        "y",
        across,
    )
    other_row = over_core(row_two.reshape(512, 384))
    side, up_two, down_two, across_two, inner, other_row = lax.optimization_barrier(
        (side, up_two, down_two, across_two, inner, other_row)
    )

    other_outer = over_core(outer[0:512])
    other_side = over_core(side[0:512])
    others = [over_core(t) for t in (up_two, down_two, across_two)]

    out = attend_call(
        place, idx_one, idx_two, rf, other, from_up, from_down,
        inner, outer, side, other_outer, other_side,
        row_two.reshape(512, 384), up_two, down_two, across_two, other_row, *others,
    )
    back = lax.all_to_all(out, "x", 0, 0, tiled=True)
    tile = call(unpack_kernel, shape(256, 768), [VMEM], nbytes=1 << 20)(back)
    return tile.reshape(16, 16, 768)


def solution(mesh):
    fine_mesh = Mesh(mesh.devices.reshape(4, 4, 8, 2), ("y", "x", "z", "core"))
    spec = P(("y", "x"), ("z", "core"), None)
    return jax.shard_map(
        body, mesh=fine_mesh, in_specs=(spec, spec, spec, P(), P()), out_specs=spec, check_vma=False
    )
```
